32 devices in a mesh: parts: 2 (over y), seq: 4 (over z), chan: 2 (over x), rep: 2 (over core).
Axes of the slice: x: 2, y: 2, z: 4, core: 2. Of those that a mesh axis runs over, the one named last changes fastest.
Arguments:
- tokens: bfloat16 [4096, 4096], P(('parts', 'seq'), ('chan', 'rep')), parts along dimension 0, may hold values from -6 to 6
- w_query: bfloat16 [4096, 4096], P('seq', ('chan', 'rep')), may hold values from -0.09375 to 0.09375
- w_key: bfloat16 [4096, 4096], P('seq', ('chan', 'rep')), may hold values from -0.09375 to 0.09375
- w_value: bfloat16 [4096, 4096], P('seq', ('chan', 'rep')), may hold values from -0.09375 to 0.09375
- decay_rate: float32 [4096, 16], P(('chan', 'rep', 'seq')), may hold values from 4.8828125e-06 to 0.04, as said below
- residue: float32 [4096, 16], P(('chan', 'rep', 'seq')), may hold values from -1.5 to 1.5
- carried: float32 [8192, 16], P(('parts', 'chan', 'rep', 'seq')), parts along dimension 0, may hold values from -6 to 6
Outputs:
- gated_output: bfloat16 [4096, 4096], P(('parts', 'seq'), ('chan', 'rep')), parts along dimension 0
- new_state: float32 [8192, 16], P(('parts', 'chan', 'rep', 'seq')), parts along dimension 0
The draws below stay inside these ranges and needn't reach their ends.
There are 2 independent parts, one for each index of `parts`. The reference program is written for one: setup_inputs(seed, part) draws one part's arguments, and reference() takes and returns one part's arrays. A program takes and returns all parts, laid end to end along the dimension named above; an argument that names none is the same for every part. Nothing has to cross between parts.
Inputs may be any that keep to these rules, and one draw needn't show every extreme that they name: `decay_rate`: each rate lies between 0.01 / 2048 and 0.04.
All inputs are finite; a program needn't handle non-finite values.
Results may differ from the reference program's by a relative error of at most 0.0066.
Values may be sent and summed in bfloat16 or wider, within the bound.
No kernel may reach another device: no remote copies, remote signals or barrier semaphores. Data moves between devices by JAX's collectives and lax.ppermute only.
A program may use at most 128 MiB of HBM per device.

```python
import math
import jax
import jax.numpy as jnp
from jax import lax

D = 4096
MODES = 16
LENGTH = 2048


def draw_decay_rate(key, part):
    lowest = 0.01 / LENGTH
    subkeys = jax.random.split(key, 1)
    return jnp.exp(jax.random.uniform(subkeys[0], (D, MODES), jnp.float32, math.log(lowest), math.log(0.04))).astype(jnp.float32)


def level_of(own_key, extent, cuts, least, top_value):
    def one(dim, parts):
        heights = jax.random.uniform(jax.random.fold_in(jax.random.fold_in(own_key, 6), dim), (parts,), jnp.float32, least / len(cuts), top_value / len(cuts))
        return jnp.repeat(jnp.exp(heights), extent[dim] // parts).reshape((-1,) + (1,) * (len(extent) - dim - 1))

    gain = one(*cuts[0])
    for cut in cuts[1:]:
        gain = gain * one(*cut)
    return gain


def noise(stream_key, extent, scale, bound, cuts=(), kind=jnp.bfloat16):
    loudness = level_of(stream_key, extent, cuts, -0.22, 0.18) if cuts else 1.0
    values = jax.random.normal(stream_key, extent, jnp.float32) * scale * loudness
    return jnp.minimum(jnp.maximum(values, -bound), bound).astype(kind)


def setup_inputs(seed: int = 0, part: int = 0) -> dict:
    key_of = jax.random.split(jax.random.key(seed), 8)
    part_keys = jax.random.split(jax.random.fold_in(key_of[7], part), 8)
    tokens = noise(part_keys[0], (LENGTH, D), 1.0, 6.0, ((0, 4), (1, 4)))
    w_query = noise(key_of[1], (D, D), D ** -0.5, 0.09375, ((0, 4), (1, 4)))
    w_key = noise(key_of[2], (D, D), D ** -0.5, 0.09375, ((0, 4), (1, 4)))
    w_value = noise(key_of[3], (D, D), D ** -0.5, 0.09375, ((0, 4), (1, 4)))
    decay_rate = draw_decay_rate(jax.random.fold_in(key_of[7], 71), part)
    residue = noise(key_of[5], (D, MODES), 0.25, 1.5, ((0, 16),), jnp.float32)
    carried = noise(part_keys[6], (D, MODES), 1.0, 6.0, ((0, 16),), jnp.float32)
    return {"tokens": tokens, "w_query": w_query, "w_key": w_key, "w_value": w_value, "decay_rate": decay_rate, "residue": residue, "carried": carried}


def channel_group(operands):
    signal, decay_rates, residues, start_state = operands
    seq_length = signal.shape[1]
    offsets = jnp.arange(seq_length, dtype=jnp.float32)
    scaling = jnp.sqrt(-jnp.expm1(-2.0 * decay_rates))
    powers = jnp.exp(-decay_rates[:, :, None] * offsets[None, None, :])
    kernel = lax.optimization_barrier(jnp.sum((residues * scaling)[:, :, None] * powers, axis=1))
    padded_size = 2 * seq_length
    spectrum = jnp.fft.rfft(signal, padded_size) * jnp.fft.rfft(kernel, padded_size)
    direct = jnp.fft.irfft(spectrum, padded_size)[:, :seq_length]
    carried_part = lax.optimization_barrier(jnp.sum((residues * start_state * jnp.exp(-decay_rates))[:, :, None] * powers, axis=1))
    final_state = jnp.exp(-decay_rates * seq_length) * start_state + scaling * lax.optimization_barrier(jnp.sum(powers[:, :, ::-1] * signal[:, None, :], axis=2))
    return (direct + carried_part, final_state)

def reference(tokens, w_query, w_key, w_value, decay_rate, residue, carried):
    query_rows = jnp.dot(tokens, w_query, preferred_element_type=jnp.float32).astype(jnp.bfloat16)
    key_rows = jnp.dot(tokens, w_key, preferred_element_type=jnp.float32).astype(jnp.bfloat16)
    value_rows = jnp.dot(tokens, w_value, preferred_element_type=jnp.float32).astype(jnp.bfloat16)
    query_rows, key_rows, value_rows = lax.optimization_barrier((query_rows, key_rows, value_rows))
    product = (key_rows.astype(jnp.float32) * value_rows.astype(jnp.float32)).astype(jnp.bfloat16)
    product = lax.optimization_barrier(product)
    signal = product.astype(jnp.float32).T
    groups = D // 256
    conv, final_state = lax.map(channel_group, (signal.reshape(groups, 256, -1), decay_rate.reshape(groups, 256, -1), residue.reshape(groups, 256, -1), carried.reshape(groups, 256, -1)))
    conv = conv.reshape(D, -1).astype(jnp.bfloat16)
    conv = lax.optimization_barrier(conv)
    gated_output = (query_rows.astype(jnp.float32) * conv.T.astype(jnp.float32)).astype(jnp.bfloat16)
    return (gated_output, final_state.reshape(D, -1))
```

```python
import jax
import jax.numpy as jnp
from jax import lax
from jax.experimental import pallas as pl
from jax.experimental.pallas import tpu as pltpu
from jax.sharding import PartitionSpec as P

BLOCK = 128
SUBLANES, LANES = 8, 128
TILE = 256
UNROLL = 4
GATHER_BYTES = 24 << 20


HIGHEST_PRECISION = lax.Precision.HIGHEST


def mode_scale(decay_rates):
    return jnp.sqrt(-jnp.expm1(-2.0 * decay_rates))


def local_ends(blocks, decay_rates):
    block_width = blocks.shape[2]
    offsets = jnp.arange(block_width, dtype=jnp.float32)
    tail_powers = jnp.exp(-decay_rates[:, :, None] * (block_width - 1.0 - offsets)[None, None, :])
    sums_here = jnp.einsum("cnb,cmb->cnm", blocks, tail_powers, precision=HIGHEST_PRECISION)
    return mode_scale(decay_rates)[:, None, :] * sums_here


def combine_states(earlier, later):
    return (earlier[0] * later[0], later[0] * earlier[1] + later[1])


def block_sums(block_ends, decay_rates, block_width):
    step_decay = jnp.broadcast_to(jnp.exp(-decay_rates * block_width)[:, None, :], block_ends.shape)
    unused_decay, running = lax.associative_scan(combine_states, (step_decay, block_ends), axis=1)
    return running


def entering_states(running, decay_rates, start_state, block_width):
    count_blocks = running.shape[1]
    block_starts = jnp.arange(count_blocks, dtype=jnp.float32) * block_width
    decayed = (
        jnp.exp(-decay_rates[:, None, :] * block_starts[None, :, None]) * start_state[:, None, :]
    )
    earlier_sums = jnp.concatenate([jnp.zeros_like(running[:, :1]), running[:, :-1]], axis=1)
    final_state = (
        jnp.exp(-decay_rates * (count_blocks * block_width)) * start_state + running[:, -1]
    )
    return (decayed + earlier_sums, final_state)


def block_convolve(blocks, decay_rates, residues, entering):
    block_width = blocks.shape[2]
    offsets = jnp.arange(block_width, dtype=jnp.float32)
    powers = jnp.exp(-decay_rates[:, :, None] * offsets[None, None, :])
    kernel = jnp.sum((residues * mode_scale(decay_rates))[:, :, None] * powers, axis=1)
    out_index = jnp.arange(block_width, dtype=jnp.int32)[:, None]
    in_index = jnp.arange(block_width, dtype=jnp.int32)[None, :]
    lag = jnp.maximum(out_index - in_index, 0)
    causal = (out_index >= in_index).astype(jnp.float32)
    toeplitz = kernel[:, lag] * causal[None, :, :]
    direct = jnp.einsum("cij,cnj->cni", toeplitz, blocks, precision=HIGHEST_PRECISION)
    leading = residues[:, :, None] * jnp.exp(
        -decay_rates[:, :, None] * (offsets + 1.0)[None, None, :]
    )
    return direct + jnp.einsum("cnm,cmb->cnb", entering, leading, precision=HIGHEST_PRECISION)


def per_device(tokens, w_query, w_key, w_value, decay_rate, residue, carried):
    gathered = lax.all_gather(tokens, ("chan", "rep"), axis=1, tiled=True)
    pieces = (
        lax.all_gather(w_query, "seq", axis=0, tiled=True),
        lax.all_gather(w_key, "seq", axis=0, tiled=True),
        lax.all_gather(w_value, "seq", axis=0, tiled=True),
    )
    query_acc, key_acc, value_acc = tuple(
        (
            lax.dot_general(
                weight_piece, gathered, (((0,), (1,)), ((), ())), preferred_element_type=jnp.float32
            )
            for weight_piece in pieces
        )
    )
    query_rows = query_acc.astype(jnp.bfloat16)
    key_rows = key_acc.astype(jnp.bfloat16)
    value_rows = value_acc.astype(jnp.bfloat16)
    query_rows, key_rows, value_rows = lax.optimization_barrier((query_rows, key_rows, value_rows))
    product = (key_rows.astype(jnp.float32) * value_rows.astype(jnp.float32)).astype(jnp.bfloat16)
    owned = lax.all_to_all(product, "seq", split_axis=0, concat_axis=1, tiled=True)
    own_chan = owned.shape[0]
    blocks = owned.astype(jnp.float32).reshape(own_chan, -1, BLOCK)
    block_end = local_ends(blocks, decay_rate)
    running = block_sums(block_end, decay_rate, BLOCK)
    entering, new_state = entering_states(running, decay_rate, carried, BLOCK)
    conv_out = (
        block_convolve(blocks, decay_rate, residue, entering)
        .reshape(own_chan, -1)
        .astype(jnp.bfloat16)
    )
    conv_back = lax.all_to_all(conv_out, "seq", split_axis=1, concat_axis=0, tiled=True)
    conv_back = lax.optimization_barrier(conv_back)
    gated_rows = (query_rows.astype(jnp.float32) * conv_back.astype(jnp.float32)).astype(
        jnp.bfloat16
    )
    return (gated_rows.T, new_state)


def ring(size, step):
    return [(i, (i + step) % size) for i in range(size)]


def gather_line(own, axis, size):
    place = lax.axis_index(axis)
    upward, downward = {0: own}, {0: own}
    for step in range(1, size):
        upward[step] = lax.ppermute(
            upward[step - 1], axis, [(i, i + 1) for i in range(step - 1, size - 1)]
        )
        downward[step] = lax.ppermute(
            downward[step - 1], axis, [(i + 1, i) for i in range(size - step)]
        )
    arrivals = []
    for i in range(size):
        order = []
        for step in range(1, size):
            if i - step >= 0:
                order.append(("up", step, i - step))
            if i + step < size:
                order.append(("down", step, i + step))
        arrivals.append(order)
    shards = [(own, place)]
    for j in range(size - 1):
        value, owner = None, jnp.int32(0)
        for i in range(size):
            way, step, origin = arrivals[i][j]
            candidate = upward[step] if way == "up" else downward[step]
            value = candidate if value is None else jnp.where(place == i, candidate, value)
            owner = jnp.where(place == i, origin, owner)
        shards.append((value, owner))
    return shards


def exchange_weights(weights, seq, parts):
    place, part = lax.axis_index("seq"), lax.axis_index("parts")
    depth = weights[0].shape[0]
    share, width = depth // parts, weights[0].shape[1] // seq

    def block(target, first_row, rows):
        return jnp.concatenate(
            [lax.dynamic_slice(w, (first_row, target * width), (rows, width)) for w in weights], axis=1
        )

    whole = jnp.zeros((seq, parts, share, width * len(weights)), weights[0].dtype)
    own = block(place, 0, depth).reshape(1, parts, share, -1)
    whole = lax.dynamic_update_slice(whole, own, (place, 0, 0, 0))
    for step in range(1, seq):
        piece = block((place + step) % seq, part * share, share)
        piece = lax.ppermute(piece, "seq", ring(seq, step))
        origin = (place - step) % seq
        whole = lax.dynamic_update_slice(whole, piece[None, None], (origin, part, 0, 0))
        for turn in range(1, parts):
            other = lax.ppermute(piece, "parts", ring(parts, turn))
            whole = lax.dynamic_update_slice(
                whole, other[None, None], (origin, (part - turn) % parts, 0, 0)
            )
    return whole.reshape(seq, depth, -1)


def gather_tokens(tokens, seq, chan, rep):
    x_place, core = lax.axis_index("chan"), lax.axis_index("rep")
    rows, width = tokens.shape
    whole = jnp.zeros((seq, chan * rep, rows, width), tokens.dtype)
    for value, owner in gather_line(tokens, "seq", seq):
        for dx in range(chan):
            over_x = lax.ppermute(value, "chan", ring(chan, dx)) if dx else value
            for dr in range(rep):
                chunk = lax.ppermute(over_x, "rep", ring(rep, dr)) if dr else over_x
                feature = ((x_place - dx) % chan) * rep + (core - dr) % rep
                whole = lax.dynamic_update_slice(whole, chunk[None, None], (owner, feature, 0, 0))
    return whole


def mode_kernel(x_hbm, w_hbm, modes_ref, conv_ref, state_ref, x_buf, w_buf, prod, out, ends, x_sem, w_sem):
    seq, quarters, rows, depth = x_buf.shape
    groups, length, lane_width = prod.shape
    channels = groups * lane_width
    modes = modes_ref.shape[1]
    w_copy = pltpu.make_async_copy(w_hbm, w_buf, w_sem)
    w_copy.start()
    copies = [pltpu.make_async_copy(x_hbm.at[i], x_buf.at[i], x_sem.at[i]) for i in range(seq)]
    for copy in copies:
        copy.start()
    w_copy.wait()
    tile = min(rows, TILE)
    for i in range(seq):
        copies[i].wait()

        @pl.loop(0, rows // tile)
        def _(t):
            at = pl.ds(pl.multiple_of(t * tile, tile), tile)
            acc = jnp.zeros((tile, 2 * channels), jnp.float32)
            for q in range(quarters):
                acc += jnp.dot(x_buf[i, q, at, :], w_buf[q], preferred_element_type=jnp.float32)
            rounded = acc.astype(jnp.bfloat16).astype(jnp.float32)
            product = (rounded[:, :channels] * rounded[:, channels:]).astype(jnp.bfloat16)
            for g in range(groups):
                prod[g, pl.ds(pl.multiple_of(i * rows + t * tile, tile), tile), :] = product[
                    :, g * LANES : (g + 1) * LANES
                ].astype(jnp.float32)

    span = length // SUBLANES
    for g in range(groups):
        lanes = pl.ds(g * LANES, LANES)
        signal, result = prod.at[g], out.at[g]
        decay = [jnp.broadcast_to(modes_ref[0, m : m + 1, lanes], (SUBLANES, LANES)) for m in range(modes)]
        weight = [jnp.broadcast_to(modes_ref[2, m : m + 1, lanes], (SUBLANES, LANES)) for m in range(modes)]

        def sums(i, states):
            for u in range(UNROLL):
                value = signal[pl.ds(i * UNROLL + u, SUBLANES, stride=span), :]
                states = tuple(a * s + value for a, s in zip(decay, states))
            return states

        zero = jnp.zeros((SUBLANES, LANES), jnp.float32)
        states = lax.fori_loop(0, span // UNROLL, sums, (zero,) * modes)
        for m in range(modes):
            ends[m] = states[m]
        state = modes_ref[3, :, lanes]
        over_span = modes_ref[1, :, lanes]
        for b in range(SUBLANES):
            end = ends[:, b, :]
            ends[:, b, :] = state
            state = over_span * state + end
        state_ref[:, lanes] = state * modes_ref[4, :, lanes]

        def outputs(i, states):
            for u in range(UNROLL):
                at = pl.ds(i * UNROLL + u, SUBLANES, stride=span)
                value = signal[at, :]
                states = tuple(a * s + value for a, s in zip(decay, states))
                terms = [w * s for w, s in zip(weight, states)]
                while len(terms) > 1:
                    terms = [sum(terms[k : k + 2][1:], terms[k]) for k in range(0, len(terms), 2)]
                result[at, :] = terms[0]
            return states

        lax.fori_loop(0, span // UNROLL, outputs, tuple(ends[m] for m in range(modes)))
        conv_ref[:, lanes] = result[...].astype(jnp.bfloat16)


def key_value_modes(x_all, w_all, decay_rate, residue, carried):
    seq, quarters, rows, depth = x_all.shape
    length, channels = seq * rows, decay_rate.shape[0]
    modes = decay_rate.shape[1]
    scale = mode_scale(decay_rate)
    table = jnp.stack(
        [
            jnp.exp(-decay_rate),
            jnp.exp(-decay_rate * (length // SUBLANES)),
            residue * scale,
            carried / scale,
            scale,
        ]
    ).transpose(0, 2, 1)
    conv, state = pl.pallas_call(
        mode_kernel,
        out_shape=(
            jax.ShapeDtypeStruct((length, channels), jnp.bfloat16),
            jax.ShapeDtypeStruct((modes, channels), jnp.float32),
        ),
        in_specs=[
            pl.BlockSpec(memory_space=pl.ANY),
            pl.BlockSpec(memory_space=pl.ANY),
            pl.BlockSpec(memory_space=pltpu.VMEM),
        ],
        out_specs=(pl.BlockSpec(memory_space=pltpu.VMEM), pl.BlockSpec(memory_space=pltpu.VMEM)),
        scratch_shapes=[
            pltpu.VMEM(x_all.shape, x_all.dtype),
            pltpu.VMEM(w_all.shape, w_all.dtype),
            pltpu.VMEM((channels // LANES, length, LANES), jnp.float32),
            pltpu.VMEM((channels // LANES, length, LANES), jnp.float32),
            pltpu.VMEM((modes, SUBLANES, LANES), jnp.float32),
            pltpu.SemaphoreType.DMA((seq,)),
            pltpu.SemaphoreType.DMA,
        ],
        compiler_params=pltpu.CompilerParams(vmem_limit_bytes=44 << 20),
        cost_estimate=pl.CostEstimate(
            flops=4 * length * depth * quarters * channels,
            bytes_accessed=2 * (x_all.size + w_all.size),
            transcendentals=0,
        ),
        name="key_value_modes",
    )(x_all, w_all, table)
    return conv, state.T


def gate_kernel(where_ref, x_ref, w_ref, conv_ref, out_ref):
    del where_ref
    quarters = x_ref.shape[1]
    acc = jnp.zeros(out_ref.shape, jnp.float32)
    for q in range(quarters):
        acc += jnp.dot(x_ref[0, q], w_ref[q], preferred_element_type=jnp.float32)
    query = acc.astype(jnp.bfloat16).astype(jnp.float32)
    out_ref[...] = (query * conv_ref[...].astype(jnp.float32)).astype(jnp.bfloat16)


def gate(x_all, w_all, conv, owner):
    seq, quarters, rows, depth = x_all.shape
    channels = conv.shape[1]
    return pl.pallas_call(
        gate_kernel,
        out_shape=jax.ShapeDtypeStruct((rows, channels), jnp.bfloat16),
        grid_spec=pltpu.PrefetchScalarGridSpec(
            num_scalar_prefetch=1,
            grid=(1,),
            in_specs=[
                pl.BlockSpec((1, quarters, rows, depth), lambda g, w: (w[0], 0, 0, 0)),
                pl.BlockSpec(w_all.shape, lambda g, w: (0, 0, 0)),
                pl.BlockSpec((rows, channels), lambda g, w: (w[0], 0)),
            ],
            out_specs=pl.BlockSpec((rows, channels), lambda g, w: (0, 0)),
        ),
        compiler_params=pltpu.CompilerParams(vmem_limit_bytes=32 << 20),
        cost_estimate=pl.CostEstimate(
            flops=2 * rows * depth * quarters * channels,
            bytes_accessed=2 * (x_all.size // seq + w_all.size),
            transcendentals=0,
        ),
        name="gate",
    )(owner.reshape(1).astype(jnp.int32), x_all, w_all, conv)


def by_channels(sizes, tokens, w_query, w_key, w_value, decay_rate, residue, carried):
    seq, chan, rep, parts = sizes["seq"], sizes["chan"], sizes["rep"], sizes["parts"]
    place = lax.axis_index("seq")
    x_all = gather_tokens(tokens, seq, chan, rep)
    w_key_value = exchange_weights((w_key, w_value), seq, parts)
    w_own_query = exchange_weights((w_query,), seq, parts)
    conv, new_state = key_value_modes(x_all, w_key_value, decay_rate, residue, carried)
    rows, channels = tokens.shape[0], decay_rate.shape[0]
    gated = jnp.zeros((seq, rows, channels), jnp.bfloat16)
    for step in sorted(range(seq), key=lambda d: -min(d, seq - d)):
        piece = gate(x_all, w_own_query, conv, (place + step) % seq)
        if step:
            piece = lax.ppermute(piece, "seq", ring(seq, step))
        gated = lax.dynamic_update_slice(gated, piece[None], ((place - step) % seq, 0, 0))
    return gated.transpose(1, 0, 2).reshape(rows, seq * channels), new_state


def solution(mesh):
    in_specs = (
        P(("parts", "seq"), ("chan", "rep")),
        P("seq", ("chan", "rep")),
        P("seq", ("chan", "rep")),
        P("seq", ("chan", "rep")),
        P(("chan", "rep", "seq"), None),
        P(("chan", "rep", "seq"), None),
        P(("parts", "chan", "rep", "seq"), None),
    )
    out_specs = (P(("parts", "seq"), ("chan", "rep")), P(("parts", "chan", "rep", "seq"), None))
    sizes = dict(mesh.shape)

    def program(*arrays):
        tokens = arrays[0]
        part_bytes = tokens.size * tokens.dtype.itemsize * sizes["seq"] * sizes["chan"] * sizes["rep"]
        fits = part_bytes <= GATHER_BYTES and sizes["seq"] == sizes["chan"] * sizes["rep"]
        if fits:
            return by_channels(sizes, *arrays)
        return per_device(*arrays)

    return jax.shard_map(
        program, mesh=mesh, in_specs=in_specs, out_specs=out_specs, check_vma=False
    )
```

```python
import jax
import jax.numpy as jnp
from jax import lax
from jax.experimental import pallas as pl
from jax.experimental.pallas import tpu as pltpu
from jax.sharding import PartitionSpec as P

BLOCK = 128
SUBLANES, LANES = 8, 128
TILE = 256
UNROLL = 4
GATHER_BYTES = 24 << 20


HIGHEST_PRECISION = lax.Precision.HIGHEST


def mode_scale(decay_rates):
    return jnp.sqrt(-jnp.expm1(-2.0 * decay_rates))


def local_ends(blocks, decay_rates):
    block_width = blocks.shape[2]
    offsets = jnp.arange(block_width, dtype=jnp.float32)
    tail_powers = jnp.exp(-decay_rates[:, :, None] * (block_width - 1.0 - offsets)[None, None, :])
    sums_here = jnp.einsum("cnb,cmb->cnm", blocks, tail_powers, precision=HIGHEST_PRECISION)
    return mode_scale(decay_rates)[:, None, :] * sums_here


def combine_states(earlier, later):
    return (earlier[0] * later[0], later[0] * earlier[1] + later[1])


def block_sums(block_ends, decay_rates, block_width):
    step_decay = jnp.broadcast_to(jnp.exp(-decay_rates * block_width)[:, None, :], block_ends.shape)
    unused_decay, running = lax.associative_scan(combine_states, (step_decay, block_ends), axis=1)
    return running


def entering_states(running, decay_rates, start_state, block_width):
    count_blocks = running.shape[1]
    block_starts = jnp.arange(count_blocks, dtype=jnp.float32) * block_width
    decayed = (
        jnp.exp(-decay_rates[:, None, :] * block_starts[None, :, None]) * start_state[:, None, :]
    )
    earlier_sums = jnp.concatenate([jnp.zeros_like(running[:, :1]), running[:, :-1]], axis=1)
    final_state = (
        jnp.exp(-decay_rates * (count_blocks * block_width)) * start_state + running[:, -1]
    )
    return (decayed + earlier_sums, final_state)


def block_convolve(blocks, decay_rates, residues, entering):
    block_width = blocks.shape[2]
    offsets = jnp.arange(block_width, dtype=jnp.float32)
    powers = jnp.exp(-decay_rates[:, :, None] * offsets[None, None, :])
    kernel = jnp.sum((residues * mode_scale(decay_rates))[:, :, None] * powers, axis=1)
    out_index = jnp.arange(block_width, dtype=jnp.int32)[:, None]
    in_index = jnp.arange(block_width, dtype=jnp.int32)[None, :]
    lag = jnp.maximum(out_index - in_index, 0)
    causal = (out_index >= in_index).astype(jnp.float32)
    toeplitz = kernel[:, lag] * causal[None, :, :]
    direct = jnp.einsum("cij,cnj->cni", toeplitz, blocks, precision=HIGHEST_PRECISION)
    leading = residues[:, :, None] * jnp.exp(
        -decay_rates[:, :, None] * (offsets + 1.0)[None, None, :]
    )
    return direct + jnp.einsum("cnm,cmb->cnb", entering, leading, precision=HIGHEST_PRECISION)


def per_device(tokens, w_query, w_key, w_value, decay_rate, residue, carried):
    gathered = lax.all_gather(tokens, ("chan", "rep"), axis=1, tiled=True)
    pieces = (
        lax.all_gather(w_query, "seq", axis=0, tiled=True),
        lax.all_gather(w_key, "seq", axis=0, tiled=True),
        lax.all_gather(w_value, "seq", axis=0, tiled=True),
    )
    query_acc, key_acc, value_acc = tuple(
        (
            lax.dot_general(
                weight_piece, gathered, (((0,), (1,)), ((), ())), preferred_element_type=jnp.float32
            )
            for weight_piece in pieces
        )
    )
    query_rows = query_acc.astype(jnp.bfloat16)
    key_rows = key_acc.astype(jnp.bfloat16)
    value_rows = value_acc.astype(jnp.bfloat16)
    query_rows, key_rows, value_rows = lax.optimization_barrier((query_rows, key_rows, value_rows))
    product = (key_rows.astype(jnp.float32) * value_rows.astype(jnp.float32)).astype(jnp.bfloat16)
    owned = lax.all_to_all(product, "seq", split_axis=0, concat_axis=1, tiled=True)
    own_chan = owned.shape[0]
    blocks = owned.astype(jnp.float32).reshape(own_chan, -1, BLOCK)
    block_end = local_ends(blocks, decay_rate)
    running = block_sums(block_end, decay_rate, BLOCK)
    entering, new_state = entering_states(running, decay_rate, carried, BLOCK)
    conv_out = (
        block_convolve(blocks, decay_rate, residue, entering)
        .reshape(own_chan, -1)
        .astype(jnp.bfloat16)
    )
    conv_back = lax.all_to_all(conv_out, "seq", split_axis=1, concat_axis=0, tiled=True)
    conv_back = lax.optimization_barrier(conv_back)
    gated_rows = (query_rows.astype(jnp.float32) * conv_back.astype(jnp.float32)).astype(
        jnp.bfloat16
    )
    return (gated_rows.T, new_state)


def ring(size, step):
    return [(i, (i + step) % size) for i in range(size)]


def exchange_weights(weights, seq, parts):
    place, part = lax.axis_index("seq"), lax.axis_index("parts")
    depth = weights[0].shape[0]
    share, width = depth // parts, weights[0].shape[1] // seq

    def block(target, first_row, rows):
        return jnp.concatenate(
            [lax.dynamic_slice(w, (first_row, target * width), (rows, width)) for w in weights], axis=1
        )

    whole = jnp.zeros((seq, parts, share, width * len(weights)), weights[0].dtype)
    own = block(place, 0, depth).reshape(1, parts, share, -1)
    whole = lax.dynamic_update_slice(whole, own, (place, 0, 0, 0))
    for step in range(1, seq):
        piece = block((place + step) % seq, part * share, share)
        piece = lax.ppermute(piece, "seq", ring(seq, step))
        origin = (place - step) % seq
        whole = lax.dynamic_update_slice(whole, piece[None, None], (origin, part, 0, 0))
        for turn in range(1, parts):
            other = lax.ppermute(piece, "parts", ring(parts, turn))
            whole = lax.dynamic_update_slice(
                whole, other[None, None], (origin, (part - turn) % parts, 0, 0)
            )
    return whole.reshape(seq, depth, -1)


def gather_tokens(tokens, seq, chan, rep):
    whole = lax.all_gather(tokens, ("seq", "chan", "rep"), axis=0)
    return whole.reshape(seq, chan * rep, *tokens.shape)


def mode_kernel(x_hbm, w_hbm, modes_ref, conv_ref, state_ref, x_buf, w_buf, prod, out, ends, x_sem, w_sem):
    seq, quarters, rows, depth = x_buf.shape
    groups, length, lane_width = prod.shape
    channels = groups * lane_width
    modes = modes_ref.shape[1]
    w_copy = pltpu.make_async_copy(w_hbm, w_buf, w_sem)
    w_copy.start()
    copies = [pltpu.make_async_copy(x_hbm.at[i], x_buf.at[i], x_sem.at[i]) for i in range(seq)]
    for copy in copies:
        copy.start()
    w_copy.wait()
    tile = min(rows, TILE)
    for i in range(seq):
        copies[i].wait()

        @pl.loop(0, rows // tile)
        def _(t):
            at = pl.ds(pl.multiple_of(t * tile, tile), tile)
            acc = jnp.zeros((tile, 2 * channels), jnp.float32)
            for q in range(quarters):
                acc += jnp.dot(x_buf[i, q, at, :], w_buf[q], preferred_element_type=jnp.float32)
            rounded = acc.astype(jnp.bfloat16).astype(jnp.float32)
            product = (rounded[:, :channels] * rounded[:, channels:]).astype(jnp.bfloat16)
            for g in range(groups):
                prod[g, pl.ds(pl.multiple_of(i * rows + t * tile, tile), tile), :] = product[
                    :, g * LANES : (g + 1) * LANES
                ].astype(jnp.float32)

    span = length // SUBLANES
    for g in range(groups):
        lanes = pl.ds(g * LANES, LANES)
        signal, result = prod.at[g], out.at[g]
        decay = [jnp.broadcast_to(modes_ref[0, m : m + 1, lanes], (SUBLANES, LANES)) for m in range(modes)]
        weight = [jnp.broadcast_to(modes_ref[2, m : m + 1, lanes], (SUBLANES, LANES)) for m in range(modes)]

        def sums(i, states):
            for u in range(UNROLL):
                value = signal[pl.ds(i * UNROLL + u, SUBLANES, stride=span), :]
                states = tuple(a * s + value for a, s in zip(decay, states))
            return states

        zero = jnp.zeros((SUBLANES, LANES), jnp.float32)
        states = lax.fori_loop(0, span // UNROLL, sums, (zero,) * modes)
        for m in range(modes):
            ends[m] = states[m]
        state = modes_ref[3, :, lanes]
        over_span = modes_ref[1, :, lanes]
        for b in range(SUBLANES):
            end = ends[:, b, :]
            ends[:, b, :] = state
            state = over_span * state + end
        state_ref[:, lanes] = state * modes_ref[4, :, lanes]

        def outputs(i, states):
            for u in range(UNROLL):
                at = pl.ds(i * UNROLL + u, SUBLANES, stride=span)
                value = signal[at, :]
                states = tuple(a * s + value for a, s in zip(decay, states))
                terms = [w * s for w, s in zip(weight, states)]
                while len(terms) > 1:
                    terms = [sum(terms[k : k + 2][1:], terms[k]) for k in range(0, len(terms), 2)]
                result[at, :] = terms[0]
            return states

        lax.fori_loop(0, span // UNROLL, outputs, tuple(ends[m] for m in range(modes)))
        conv_ref[:, lanes] = result[...].astype(jnp.bfloat16)


def key_value_modes(x_all, w_all, decay_rate, residue, carried):
    seq, quarters, rows, depth = x_all.shape
    length, channels = seq * rows, decay_rate.shape[0]
    modes = decay_rate.shape[1]
    scale = mode_scale(decay_rate)
    table = jnp.stack(
        [
            jnp.exp(-decay_rate),
            jnp.exp(-decay_rate * (length // SUBLANES)),
            residue * scale,
            carried / scale,
            scale,
        ]
    ).transpose(0, 2, 1)
    conv, state = pl.pallas_call(
        mode_kernel,
        out_shape=(
            jax.ShapeDtypeStruct((length, channels), jnp.bfloat16),
            jax.ShapeDtypeStruct((modes, channels), jnp.float32),
        ),
        in_specs=[
            pl.BlockSpec(memory_space=pl.ANY),
            pl.BlockSpec(memory_space=pl.ANY),
            pl.BlockSpec(memory_space=pltpu.VMEM),
        ],
        out_specs=(pl.BlockSpec(memory_space=pltpu.VMEM), pl.BlockSpec(memory_space=pltpu.VMEM)),
        scratch_shapes=[
            pltpu.VMEM(x_all.shape, x_all.dtype),
            pltpu.VMEM(w_all.shape, w_all.dtype),
            pltpu.VMEM((channels // LANES, length, LANES), jnp.float32),
            pltpu.VMEM((channels // LANES, length, LANES), jnp.float32),
            pltpu.VMEM((modes, SUBLANES, LANES), jnp.float32),
            pltpu.SemaphoreType.DMA((seq,)),
            pltpu.SemaphoreType.DMA,
        ],
        compiler_params=pltpu.CompilerParams(vmem_limit_bytes=44 << 20),
        cost_estimate=pl.CostEstimate(
            flops=4 * length * depth * quarters * channels,
            bytes_accessed=2 * (x_all.size + w_all.size),
            transcendentals=0,
        ),
        name="key_value_modes",
    )(x_all, w_all, table)
    return conv, state.T


def gate_kernel(where_ref, x_ref, w_ref, conv_ref, out_ref):
    del where_ref
    quarters = x_ref.shape[1]
    acc = jnp.zeros(out_ref.shape, jnp.float32)
    for q in range(quarters):
        acc += jnp.dot(x_ref[0, q], w_ref[q], preferred_element_type=jnp.float32)
    query = acc.astype(jnp.bfloat16).astype(jnp.float32)
    out_ref[...] = (query * conv_ref[...].astype(jnp.float32)).astype(jnp.bfloat16)


def gate(x_all, w_all, conv, owner):
    seq, quarters, rows, depth = x_all.shape
    channels = conv.shape[1]
    return pl.pallas_call(
        gate_kernel,
        out_shape=jax.ShapeDtypeStruct((rows, channels), jnp.bfloat16),
        grid_spec=pltpu.PrefetchScalarGridSpec(
            num_scalar_prefetch=1,
            grid=(1,),
            in_specs=[
                pl.BlockSpec((1, quarters, rows, depth), lambda g, w: (w[0], 0, 0, 0)),
                pl.BlockSpec(w_all.shape, lambda g, w: (0, 0, 0)),
                pl.BlockSpec((rows, channels), lambda g, w: (w[0], 0)),
            ],
            out_specs=pl.BlockSpec((rows, channels), lambda g, w: (0, 0)),
        ),
        compiler_params=pltpu.CompilerParams(vmem_limit_bytes=32 << 20),
        cost_estimate=pl.CostEstimate(
            flops=2 * rows * depth * quarters * channels,
            bytes_accessed=2 * (x_all.size // seq + w_all.size),
            transcendentals=0,
        ),
        name="gate",
    )(owner.reshape(1).astype(jnp.int32), x_all, w_all, conv)


def by_channels(sizes, tokens, w_query, w_key, w_value, decay_rate, residue, carried):
    seq, chan, rep, parts = sizes["seq"], sizes["chan"], sizes["rep"], sizes["parts"]
    place = lax.axis_index("seq")
    x_all = gather_tokens(tokens, seq, chan, rep)
    w_key_value = exchange_weights((w_key, w_value), seq, parts)
    w_own_query = exchange_weights((w_query,), seq, parts)
    conv, new_state = key_value_modes(x_all, w_key_value, decay_rate, residue, carried)
    rows, channels = tokens.shape[0], decay_rate.shape[0]
    gated = jnp.zeros((seq, rows, channels), jnp.bfloat16)
    for step in sorted(range(seq), key=lambda d: -min(d, seq - d)):
        piece = gate(x_all, w_own_query, conv, (place + step) % seq)
        if step:
            piece = lax.ppermute(piece, "seq", ring(seq, step))
        gated = lax.dynamic_update_slice(gated, piece[None], ((place - step) % seq, 0, 0))
    return gated.transpose(1, 0, 2).reshape(rows, seq * channels), new_state


def solution(mesh):
    in_specs = (
        P(("parts", "seq"), ("chan", "rep")),
        P("seq", ("chan", "rep")),
        P("seq", ("chan", "rep")),
        P("seq", ("chan", "rep")),
        P(("chan", "rep", "seq"), None),
        P(("chan", "rep", "seq"), None),
        P(("parts", "chan", "rep", "seq"), None),
    )
    out_specs = (P(("parts", "seq"), ("chan", "rep")), P(("parts", "chan", "rep", "seq"), None))
    sizes = dict(mesh.shape)

    def program(*arrays):
        tokens = arrays[0]
        part_bytes = tokens.size * tokens.dtype.itemsize * sizes["seq"] * sizes["chan"] * sizes["rep"]
        fits = part_bytes <= GATHER_BYTES and sizes["seq"] == sizes["chan"] * sizes["rep"]
        if fits:
            return by_channels(sizes, *arrays)
        return per_device(*arrays)

    return jax.shard_map(
        program, mesh=mesh, in_specs=in_specs, out_specs=out_specs, check_vma=False
    )
```

```python
import functools

import jax
import jax.numpy as jnp
from jax import lax
from jax.experimental import pallas as pl
from jax.experimental.pallas import tpu as pltpu
from jax.sharding import PartitionSpec as P

BLOCK = 128
SUBLANES, LANES = 8, 128
TILE = 256
UNROLL = 4
GATHER_BYTES = 24 << 20
KERNEL_BYTES = 56 << 20
FINISH_COST = 4


HIGHEST_PRECISION = lax.Precision.HIGHEST


def mode_scale(decay_rates):
    return jnp.sqrt(-jnp.expm1(-2.0 * decay_rates))


def local_ends(blocks, decay_rates):
    block_width = blocks.shape[2]
    offsets = jnp.arange(block_width, dtype=jnp.float32)
    tail_powers = jnp.exp(-decay_rates[:, :, None] * (block_width - 1.0 - offsets)[None, None, :])
    sums_here = jnp.einsum("cnb,cmb->cnm", blocks, tail_powers, precision=HIGHEST_PRECISION)
    return mode_scale(decay_rates)[:, None, :] * sums_here


def combine_states(earlier, later):
    return (earlier[0] * later[0], later[0] * earlier[1] + later[1])


def block_sums(block_ends, decay_rates, block_width):
    step_decay = jnp.broadcast_to(jnp.exp(-decay_rates * block_width)[:, None, :], block_ends.shape)
    unused_decay, running = lax.associative_scan(combine_states, (step_decay, block_ends), axis=1)
    return running


def entering_states(running, decay_rates, start_state, block_width):
    count_blocks = running.shape[1]
    block_starts = jnp.arange(count_blocks, dtype=jnp.float32) * block_width
    decayed = (
        jnp.exp(-decay_rates[:, None, :] * block_starts[None, :, None]) * start_state[:, None, :]
    )
    earlier_sums = jnp.concatenate([jnp.zeros_like(running[:, :1]), running[:, :-1]], axis=1)
    final_state = (
        jnp.exp(-decay_rates * (count_blocks * block_width)) * start_state + running[:, -1]
    )
    return (decayed + earlier_sums, final_state)


def block_convolve(blocks, decay_rates, residues, entering):
    block_width = blocks.shape[2]
    offsets = jnp.arange(block_width, dtype=jnp.float32)
    powers = jnp.exp(-decay_rates[:, :, None] * offsets[None, None, :])
    kernel = jnp.sum((residues * mode_scale(decay_rates))[:, :, None] * powers, axis=1)
    out_index = jnp.arange(block_width, dtype=jnp.int32)[:, None]
    in_index = jnp.arange(block_width, dtype=jnp.int32)[None, :]
    lag = jnp.maximum(out_index - in_index, 0)
    causal = (out_index >= in_index).astype(jnp.float32)
    toeplitz = kernel[:, lag] * causal[None, :, :]
    direct = jnp.einsum("cij,cnj->cni", toeplitz, blocks, precision=HIGHEST_PRECISION)
    leading = residues[:, :, None] * jnp.exp(
        -decay_rates[:, :, None] * (offsets + 1.0)[None, None, :]
    )
    return direct + jnp.einsum("cnm,cmb->cnb", entering, leading, precision=HIGHEST_PRECISION)


def per_device(tokens, w_query, w_key, w_value, decay_rate, residue, carried):
    gathered = lax.all_gather(tokens, ("chan", "rep"), axis=1, tiled=True)
    pieces = (
        lax.all_gather(w_query, "seq", axis=0, tiled=True),
        lax.all_gather(w_key, "seq", axis=0, tiled=True),
        lax.all_gather(w_value, "seq", axis=0, tiled=True),
    )
    query_acc, key_acc, value_acc = tuple(
        (
            lax.dot_general(
                weight_piece, gathered, (((0,), (1,)), ((), ())), preferred_element_type=jnp.float32
            )
            for weight_piece in pieces
        )
    )
    query_rows = query_acc.astype(jnp.bfloat16)
    key_rows = key_acc.astype(jnp.bfloat16)
    value_rows = value_acc.astype(jnp.bfloat16)
    query_rows, key_rows, value_rows = lax.optimization_barrier((query_rows, key_rows, value_rows))
    product = (key_rows.astype(jnp.float32) * value_rows.astype(jnp.float32)).astype(jnp.bfloat16)
    owned = lax.all_to_all(product, "seq", split_axis=0, concat_axis=1, tiled=True)
    own_chan = owned.shape[0]
    blocks = owned.astype(jnp.float32).reshape(own_chan, -1, BLOCK)
    block_end = local_ends(blocks, decay_rate)
    running = block_sums(block_end, decay_rate, BLOCK)
    entering, new_state = entering_states(running, decay_rate, carried, BLOCK)
    conv_out = (
        block_convolve(blocks, decay_rate, residue, entering)
        .reshape(own_chan, -1)
        .astype(jnp.bfloat16)
    )
    conv_back = lax.all_to_all(conv_out, "seq", split_axis=1, concat_axis=0, tiled=True)
    conv_back = lax.optimization_barrier(conv_back)
    gated_rows = (query_rows.astype(jnp.float32) * conv_back.astype(jnp.float32)).astype(
        jnp.bfloat16
    )
    return (gated_rows.T, new_state)


def ring(size, step):
    return [(i, (i + step) % size) for i in range(size)]


def mirror(size, step):
    return [(i, i ^ step) for i in range(size)]


def after(x, *earlier):
    for other in earlier:
        if other is not None:
            probe = lax.slice(other, [n - 1 for n in other.shape], other.shape).reshape(())
            x = jnp.where(probe != probe, jnp.zeros((), x.dtype), x)
    return x


def arrival_order(size):
    orders = []
    for i in range(size):
        order = []
        for step in range(1, size):
            if i - step >= 0:
                order.append((0, step, i - step))
            if i + step < size:
                order.append((1, step, i + step))
        orders.append(order)
    return orders


def exchange_weights(weight, sizes):
    seq, parts = sizes["seq"], sizes["parts"]
    place, part = lax.axis_index("seq"), lax.axis_index("parts")
    depth, width = weight.shape[0], weight.shape[1] // seq
    share = depth // parts
    mine = lax.dynamic_slice(weight, (part * share, 0), (share, weight.shape[1]))
    mine = mine.reshape(share, seq, width).transpose(1, 0, 2)
    mine = lax.all_to_all(mine, "seq", split_axis=0, concat_axis=0, tiled=True)
    fetched = jnp.concatenate(
        [lax.dynamic_slice(mine, (place ^ step, 0, 0), (1, share, width)) for step in range(1, seq)]
    )
    shares = [mine]
    for turn in range(1, parts):
        first = (part - turn) % parts * share
        own = lax.dynamic_slice(weight, (first, place * width), (share, width))
        shares.append(jnp.concatenate([own[None], lax.ppermute(fetched, "parts", ring(parts, turn))]))
    return shares


def weight_copies(order_ref, w_hbm, w_buf, w_sem):
    quarters, share, width = w_hbm[0].shape
    parts = w_buf.shape[0] // (quarters * share)
    copies = []
    for k, ref in enumerate(w_hbm):
        columns = pl.ds(k // parts * width, width)
        shift = order_ref[quarters + k % parts] * share
        for q in range(quarters):
            at = pl.ds(pl.multiple_of(q * parts * share + shift, share), share)
            block = order_ref[q] if k % parts == 0 else order_ref[quarters + parts + q]
            copies.append(pltpu.make_async_copy(ref.at[block], w_buf.at[at, columns], w_sem.at[k, q]))
    return copies


def token_copies(x_hbm, x_buf, x_sem):
    some, rows, depth = x_hbm[0].shape
    return [
        pltpu.make_async_copy(
            x_hbm[e].at[f], x_buf.at[:, pl.ds((e * some + f) * depth, depth)], x_sem.at[e * some + f]
        )
        for e in range(len(x_hbm))
        for f in range(some)
    ]


def modes_over_time(modes_ref, prod, out, ends, conv_ref, state_ref):
    groups, length, lane_width = prod.shape
    modes = modes_ref.shape[1]
    span = length // SUBLANES
    zero = jnp.zeros((SUBLANES, LANES), jnp.float32)
    for g in range(groups):
        lanes = pl.ds(g * LANES, LANES)
        signal, result = prod.at[g], out.at[g]
        decay = [jnp.broadcast_to(modes_ref[0, m : m + 1, lanes], (SUBLANES, LANES)) for m in range(modes)]
        weight = [jnp.broadcast_to(modes_ref[2, m : m + 1, lanes], (SUBLANES, LANES)) for m in range(modes)]

        def sums(i, states):
            for u in range(UNROLL):
                value = signal[pl.ds(i * UNROLL + u, SUBLANES, stride=span), :]
                states = tuple(a * s + value for a, s in zip(decay, states))
            return states

        states = lax.fori_loop(0, span // UNROLL, sums, (zero,) * modes)
        for m in range(modes):
            ends[m] = states[m]
        state = modes_ref[3, :, lanes]
        over_span = modes_ref[1, :, lanes]
        for b in range(SUBLANES):
            end = ends[:, b, :]
            ends[:, b, :] = state
            state = over_span * state + end
        state_ref[:, lanes] = state * modes_ref[4, :, lanes]

        def outputs(i, states):
            for u in range(UNROLL):
                at = pl.ds(i * UNROLL + u, SUBLANES, stride=span)
                value = signal[at, :]
                states = tuple(a * s + value for a, s in zip(decay, states))
                terms = [w * s for w, s in zip(weight, states)]
                while len(terms) > 1:
                    terms = [sum(terms[k : k + 2][1:], terms[k]) for k in range(0, len(terms), 2)]
                result[at, :] = terms[0]
            return states

        lax.fori_loop(0, span // UNROLL, outputs, tuple(ends[m] for m in range(modes)))
        conv_ref[:, lanes] = result[...].astype(jnp.bfloat16)


def finish_kernel(n_weights, seq, order_ref, modes_ref, *refs):
    refs = list(refs)

    def take(count):
        taken = refs[:count]
        del refs[:count]
        return taken

    pair_hbm, query_hbm = take(2 * n_weights), take(n_weights)
    each = (len(refs) - 11 - seq) // seq
    x_hbm = [take(each) for _ in range(seq)]
    outs, (state_ref,) = take(seq), take(1)
    x_buf, pair_buf, query_buf, prod, out, ends, conv_buf, x_sem, pair_sem, query_sem = take(10)
    rows = x_buf.shape[1]
    channels = conv_buf.shape[1]
    groups = prod.shape[0]
    first = 2 * pair_sem.shape[1] + n_weights
    x_copies = [token_copies(x_hbm[i], x_buf.at[i], x_sem.at[i]) for i in range(seq)]
    pair_copies = weight_copies(order_ref, pair_hbm, pair_buf, pair_sem)
    query_copies = weight_copies(order_ref, query_hbm, query_buf, query_sem)
    for copy in pair_copies + x_copies[0] + x_copies[1]:
        copy.start()
    for copy in pair_copies:
        copy.wait()
    for i in range(seq):
        for copy in x_copies[i]:
            copy.wait()
        for copy in x_copies[i + 2] if i + 2 < seq else query_copies if i + 2 == seq else ():
            copy.start()
        acc = jnp.dot(x_buf[i], pair_buf[...], preferred_element_type=jnp.float32)
        rounded = acc.astype(jnp.bfloat16).astype(jnp.float32)
        product = (rounded[:, :channels] * rounded[:, channels:]).astype(jnp.bfloat16)
        to = pl.ds(pl.multiple_of(order_ref[first + i] * rows, rows), rows)
        for g in range(groups):
            prod[g, to, :] = product[:, g * LANES : (g + 1) * LANES].astype(jnp.float32)
    modes_over_time(modes_ref, prod, out, ends, conv_buf, state_ref)
    for copy in query_copies:
        copy.wait()
    for i in range(seq):
        shard = order_ref[first + i]
        acc = jnp.dot(x_buf[i], query_buf[...], preferred_element_type=jnp.float32)
        query = acc.astype(jnp.bfloat16).astype(jnp.float32)
        conv = conv_buf[pl.ds(pl.multiple_of(shard * rows, rows), rows), :].astype(jnp.float32)
        gated = (query * conv).astype(jnp.bfloat16)
        for step in range(seq):

            @pl.when(order_ref[first + seq + i] == step)
            def _():
                outs[step][...] = gated


def finish(order, xs, pair, query, decay_rate, residue, carried):
    quarters, share, width = query[0].shape
    seq = len(xs)
    rows, depth = xs[0][0].shape[1:]
    length, modes = seq * rows, decay_rate.shape[1]
    scale = mode_scale(decay_rate)
    table = jnp.stack(
        [
            jnp.exp(-decay_rate),
            jnp.exp(-decay_rate * (length // SUBLANES)),
            residue * scale,
            carried / scale,
            scale,
        ]
    ).transpose(0, 2, 1)
    vmem, anywhere = pl.BlockSpec(memory_space=pltpu.VMEM), pl.BlockSpec(memory_space=pl.ANY)
    arrays = [*pair, *query, *sum(xs, [])]
    *gated, state = pl.pallas_call(
        functools.partial(finish_kernel, len(query), seq),
        out_shape=tuple(jax.ShapeDtypeStruct((rows, width), jnp.bfloat16) for _ in range(seq))
        + (jax.ShapeDtypeStruct((modes, width), jnp.float32),),
        in_specs=[pl.BlockSpec(memory_space=pltpu.SMEM), vmem]
        + [anywhere] * len(arrays),
        out_specs=(vmem,) * (seq + 1),
        scratch_shapes=[
            pltpu.VMEM((seq, rows, quarters * depth), jnp.bfloat16),
            pltpu.VMEM((quarters * depth, 2 * width), jnp.bfloat16),
            pltpu.VMEM((quarters * depth, width), jnp.bfloat16),
            pltpu.VMEM((width // LANES, length, LANES), jnp.float32),
            pltpu.VMEM((width // LANES, length, LANES), jnp.float32),
            pltpu.VMEM((modes, SUBLANES, LANES), jnp.float32),
            pltpu.VMEM((length, width), jnp.bfloat16),
            pltpu.SemaphoreType.DMA((seq, quarters)),
            pltpu.SemaphoreType.DMA((len(pair), quarters)),
            pltpu.SemaphoreType.DMA((len(query), quarters)),
        ],
        compiler_params=pltpu.CompilerParams(vmem_limit_bytes=KERNEL_BYTES),
        cost_estimate=pl.CostEstimate(
            flops=FINISH_COST * length * quarters * depth * width,
            bytes_accessed=2 * quarters * depth * (length + 3 * width),
            transcendentals=0,
        ),
        name="finish",
    )(order, table, *arrays)
    return gated, state.T


def place_columns(pieces, place):
    seq = len(pieces)
    rows, width = pieces[0].shape

    def kernel(place_ref, *refs):
        out_ref = refs[-1]
        for step in range(seq):
            origin = place_ref[0] ^ step
            out_ref[:, pl.ds(pl.multiple_of(origin * width, width), width)] = refs[step][...]

    return pl.pallas_call(
        kernel,
        out_shape=jax.ShapeDtypeStruct((rows, seq * width), pieces[0].dtype),
        in_specs=[pl.BlockSpec(memory_space=pltpu.SMEM)] + [pl.BlockSpec(memory_space=pltpu.VMEM)] * seq,
        out_specs=pl.BlockSpec(memory_space=pltpu.VMEM),
        name="place_columns",
    )(place.reshape(1).astype(jnp.int32), *pieces)


def by_channels(sizes, tokens, w_query, w_key, w_value, decay_rate, residue, carried):
    seq, chan, rep, parts = sizes["seq"], sizes["chan"], sizes["rep"], sizes["parts"]
    place, x_place, core = lax.axis_index("seq"), lax.axis_index("chan"), lax.axis_index("rep")
    orders = arrival_order(seq)

    def at_place(choices):
        value = choices[0]
        for i in range(1, seq):
            value = jnp.where(place == i, choices[i], value)
        return value

    w_keys, w_values, w_queries = [exchange_weights(w, sizes) for w in (w_key, w_value, w_query)]
    before = {2: w_keys[:1], 3: w_keys[1:] + w_values[:1], 4: w_values[1:]}
    shares = [(lax.axis_index("parts") - turn) % parts for turn in range(parts)]
    features = [
        ((x_place - turn) % chan) * rep + (core - other) % rep for other in range(rep) for turn in range(chan)
    ]
    by_feature = jnp.stack([jnp.int32(i) for i in features + shares + [f ^ place for f in features]])
    arrival, ways, xs, origins, last = tokens, [{0: tokens}, {0: tokens}], [], [place], None
    for phase in range(1, seq + 1):
        group = [arrival]
        for turn in range(1, chan):
            last = lax.ppermute(after(arrival, last, *before.get(phase, ())), "chan", ring(chan, turn))
            group.append(last)
        if phase == seq:
            group[-1] = after(group[-1], *w_queries[1:])
        both = jnp.stack(group)
        xs.append([both] + [lax.ppermute(both, "rep", ring(rep, turn)) for turn in range(1, rep)])
        if phase == seq:
            break
        ups = [(i, i + 1) for i in range(phase - 1, seq - 1)]
        downs = [(i + 1, i) for i in range(seq - phase)]
        ways[0][phase] = lax.ppermute(ways[0][phase - 1], "seq", ups)
        ways[1][phase] = lax.ppermute(ways[1][phase - 1], "seq", downs)
        chosen = [orders[i][phase - 1] for i in range(seq)]
        arrival = at_place([ways[way][step] for way, step, origin in chosen])
        origins.append(at_place([jnp.int32(origin) for way, step, origin in chosen]))

    steps = [place ^ origin for origin in origins]
    order = jnp.concatenate([by_feature, jnp.stack([jnp.int32(i) for i in origins + steps])])

    gated, new_state = finish(order, xs, w_keys + w_values, w_queries, decay_rate, residue, carried)
    pieces = [
        lax.ppermute(gated[step], "seq", mirror(seq, step)) if step else gated[0] for step in range(seq)
    ]
    return place_columns(pieces, place), new_state


def solution(mesh):
    in_specs = (
        P(("parts", "seq"), ("chan", "rep")),
        P("seq", ("chan", "rep")),
        P("seq", ("chan", "rep")),
        P("seq", ("chan", "rep")),
        P(("chan", "rep", "seq"), None),
        P(("chan", "rep", "seq"), None),
        P(("parts", "chan", "rep", "seq"), None),
    )
    out_specs = (P(("parts", "seq"), ("chan", "rep")), P(("parts", "chan", "rep", "seq"), None))
    sizes = dict(mesh.shape)

    def program(*arrays):
        tokens = arrays[0]
        part_bytes = tokens.size * tokens.dtype.itemsize * sizes["seq"] * sizes["chan"] * sizes["rep"]
        seq = sizes["seq"]
        fits = part_bytes <= GATHER_BYTES and seq == sizes["chan"] * sizes["rep"]
        fits = fits and seq >= 4 and seq & (seq - 1) == 0
        if fits:
            return by_channels(sizes, *arrays)
        return per_device(*arrays)

    return jax.shard_map(
        program, mesh=mesh, in_specs=in_specs, out_specs=out_specs, check_vma=False
    )
```

```python
import functools

import jax
import jax.numpy as jnp
from jax import lax
from jax.experimental import pallas as pl
from jax.experimental.pallas import tpu as pltpu
from jax.sharding import PartitionSpec as P

BLOCK = 128
SUBLANES, LANES = 8, 128
TILE = 256
UNROLL = 8
GATHER_BYTES = 24 << 20
KERNEL_BYTES = 56 << 20
FINISH_COST = 4
WEIGHT = 23 * 10**9


HIGHEST_PRECISION = lax.Precision.HIGHEST


def mode_scale(decay_rates):
    return jnp.sqrt(-jnp.expm1(-2.0 * decay_rates))


def local_ends(blocks, decay_rates):
    block_width = blocks.shape[2]
    offsets = jnp.arange(block_width, dtype=jnp.float32)
    tail_powers = jnp.exp(-decay_rates[:, :, None] * (block_width - 1.0 - offsets)[None, None, :])
    sums_here = jnp.einsum("cnb,cmb->cnm", blocks, tail_powers, precision=HIGHEST_PRECISION)
    return mode_scale(decay_rates)[:, None, :] * sums_here


def combine_states(earlier, later):
    return (earlier[0] * later[0], later[0] * earlier[1] + later[1])


def block_sums(block_ends, decay_rates, block_width):
    step_decay = jnp.broadcast_to(jnp.exp(-decay_rates * block_width)[:, None, :], block_ends.shape)
    unused_decay, running = lax.associative_scan(combine_states, (step_decay, block_ends), axis=1)
    return running


def entering_states(running, decay_rates, start_state, block_width):
    count_blocks = running.shape[1]
    block_starts = jnp.arange(count_blocks, dtype=jnp.float32) * block_width
    decayed = (
        jnp.exp(-decay_rates[:, None, :] * block_starts[None, :, None]) * start_state[:, None, :]
    )
    earlier_sums = jnp.concatenate([jnp.zeros_like(running[:, :1]), running[:, :-1]], axis=1)
    final_state = (
        jnp.exp(-decay_rates * (count_blocks * block_width)) * start_state + running[:, -1]
    )
    return (decayed + earlier_sums, final_state)


def block_convolve(blocks, decay_rates, residues, entering):
    block_width = blocks.shape[2]
    offsets = jnp.arange(block_width, dtype=jnp.float32)
    powers = jnp.exp(-decay_rates[:, :, None] * offsets[None, None, :])
    kernel = jnp.sum((residues * mode_scale(decay_rates))[:, :, None] * powers, axis=1)
    out_index = jnp.arange(block_width, dtype=jnp.int32)[:, None]
    in_index = jnp.arange(block_width, dtype=jnp.int32)[None, :]
    lag = jnp.maximum(out_index - in_index, 0)
    causal = (out_index >= in_index).astype(jnp.float32)
    toeplitz = kernel[:, lag] * causal[None, :, :]
    direct = jnp.einsum("cij,cnj->cni", toeplitz, blocks, precision=HIGHEST_PRECISION)
    leading = residues[:, :, None] * jnp.exp(
        -decay_rates[:, :, None] * (offsets + 1.0)[None, None, :]
    )
    return direct + jnp.einsum("cnm,cmb->cnb", entering, leading, precision=HIGHEST_PRECISION)


def per_device(tokens, w_query, w_key, w_value, decay_rate, residue, carried):
    gathered = lax.all_gather(tokens, ("chan", "rep"), axis=1, tiled=True)
    pieces = (
        lax.all_gather(w_query, "seq", axis=0, tiled=True),
        lax.all_gather(w_key, "seq", axis=0, tiled=True),
        lax.all_gather(w_value, "seq", axis=0, tiled=True),
    )
    query_acc, key_acc, value_acc = tuple(
        (
            lax.dot_general(
                weight_piece, gathered, (((0,), (1,)), ((), ())), preferred_element_type=jnp.float32
            )
            for weight_piece in pieces
        )
    )
    query_rows = query_acc.astype(jnp.bfloat16)
    key_rows = key_acc.astype(jnp.bfloat16)
    value_rows = value_acc.astype(jnp.bfloat16)
    query_rows, key_rows, value_rows = lax.optimization_barrier((query_rows, key_rows, value_rows))
    product = (key_rows.astype(jnp.float32) * value_rows.astype(jnp.float32)).astype(jnp.bfloat16)
    owned = lax.all_to_all(product, "seq", split_axis=0, concat_axis=1, tiled=True)
    own_chan = owned.shape[0]
    blocks = owned.astype(jnp.float32).reshape(own_chan, -1, BLOCK)
    block_end = local_ends(blocks, decay_rate)
    running = block_sums(block_end, decay_rate, BLOCK)
    entering, new_state = entering_states(running, decay_rate, carried, BLOCK)
    conv_out = (
        block_convolve(blocks, decay_rate, residue, entering)
        .reshape(own_chan, -1)
        .astype(jnp.bfloat16)
    )
    conv_back = lax.all_to_all(conv_out, "seq", split_axis=1, concat_axis=0, tiled=True)
    conv_back = lax.optimization_barrier(conv_back)
    gated_rows = (query_rows.astype(jnp.float32) * conv_back.astype(jnp.float32)).astype(
        jnp.bfloat16
    )
    return (gated_rows.T, new_state)


def ring(size, step):
    return [(i, (i + step) % size) for i in range(size)]


def mirror(size, step):
    return [(i, i ^ step) for i in range(size)]


def choose(index, candidates, waits, weight=0):
    shape = candidates[0]

    def kernel(index_ref, *refs):
        for i in range(len(candidates)):

            @pl.when(index_ref[0] == i)
            def _():
                refs[-1][...] = refs[i][...]

    vmem = pl.BlockSpec(memory_space=pltpu.VMEM)
    return pl.pallas_call(
        kernel,
        out_shape=jax.ShapeDtypeStruct(shape.shape, shape.dtype),
        in_specs=[pl.BlockSpec(memory_space=pltpu.SMEM)]
        + [vmem] * len(candidates)
        + [pl.BlockSpec(memory_space=pl.ANY)] * len(waits),
        out_specs=vmem,
        cost_estimate=pl.CostEstimate(flops=weight, bytes_accessed=2 * shape.size, transcendentals=0),
        name="choose",
    )(index.reshape(1).astype(jnp.int32), *candidates, *waits)


def after(x, *waits):
    def nothing(*refs):
        del refs

    anywhere = pl.BlockSpec(memory_space=pl.ANY)
    return pl.pallas_call(
        nothing,
        out_shape=jax.ShapeDtypeStruct(x.shape, x.dtype),
        in_specs=[anywhere] * (1 + len(waits)),
        out_specs=anywhere,
        input_output_aliases={0: 0},
        name="after",
    )(x, *waits)


def arrival_order(size):
    orders = []
    for i in range(size):
        order = []
        for step in range(1, size):
            if i - step >= 0:
                order.append((0, step, i - step))
            if i + step < size:
                order.append((1, step, i + step))
        orders.append(order)
    return orders


def exchange_weights(weight, sizes):
    seq, parts = sizes["seq"], sizes["parts"]
    place, part = lax.axis_index("seq"), lax.axis_index("parts")
    depth, width = weight.shape[0], weight.shape[1] // seq
    share = depth // parts
    mine = jnp.stack(
        [lax.dynamic_slice(weight, (part * share, i * width), (share, width)) for i in range(seq)]
    )
    mine = lax.all_to_all(mine, "seq", split_axis=0, concat_axis=0, tiled=True)
    fetched = jnp.concatenate(
        [lax.dynamic_slice(mine, (place ^ step, 0, 0), (1, share, width)) for step in range(1, seq)]
    )
    shares = [mine]
    for turn in range(1, parts):
        first = (part - turn) % parts * share
        own = lax.dynamic_slice(weight, (first, place * width), (share, width))
        shares += [own, lax.ppermute(fetched, "parts", ring(parts, turn))]
    return shares


def weight_copies(order_ref, w_hbm, w_buf, w_sem):
    quarters, share, width = w_hbm[0].shape
    parts = w_buf.shape[0] // (quarters * share)
    each = 2 * parts - 1
    copies = []

    def add(source, k, quarter, turn, index):
        row = quarter * (parts * share) + order_ref[quarters + turn] * share
        at = w_buf.at[pl.ds(pl.multiple_of(row, share), share), pl.ds(k * width, width)]
        copies.append(pltpu.make_async_copy(source, at, w_sem.at[k * parts + turn, index]))

    for k in range(len(w_hbm) // each):
        mine, *others = w_hbm[k * each : (k + 1) * each]
        for q in range(quarters):
            add(mine.at[order_ref[q]], k, q, 0, q)
        for turn in range(1, parts):
            own, fetched = others[2 * turn - 2 : 2 * turn]
            for step in range(quarters):
                source = fetched.at[step - 1] if step else own
                add(source, k, order_ref[quarters + parts + step], turn, step)
    return copies


def token_copies(x_hbm, x_buf, x_sem):
    some, rows, depth = x_hbm[0].shape
    return [
        pltpu.make_async_copy(
            x_hbm[e].at[f], x_buf.at[:, pl.ds((e * some + f) * depth, depth)], x_sem.at[e * some + f]
        )
        for e in range(len(x_hbm))
        for f in range(some)
    ]


def modes_over_time(modes_ref, prod, out, ends, conv_ref, state_ref):
    groups, length, lane_width = prod.shape
    modes = modes_ref.shape[1]
    span = length // SUBLANES
    zero = jnp.zeros((SUBLANES, LANES), jnp.float32)
    for g in range(groups):
        lanes = pl.ds(g * LANES, LANES)
        signal, result = prod.at[g], out.at[g]
        decay = [jnp.broadcast_to(modes_ref[0, m : m + 1, lanes], (SUBLANES, LANES)) for m in range(modes)]
        weight = [jnp.broadcast_to(modes_ref[2, m : m + 1, lanes], (SUBLANES, LANES)) for m in range(modes)]

        def sums(i, states):
            for u in range(UNROLL):
                value = signal[pl.ds(i * UNROLL + u, SUBLANES, stride=span), :]
                states = tuple(a * s + value for a, s in zip(decay, states))
            return states

        states = lax.fori_loop(0, span // UNROLL, sums, (zero,) * modes)
        for m in range(modes):
            ends[m] = states[m]
        state = modes_ref[3, :, lanes]
        over_span = modes_ref[1, :, lanes]
        for b in range(SUBLANES):
            end = ends[:, b, :]
            ends[:, b, :] = state
            state = over_span * state + end
        state_ref[:, lanes] = state * modes_ref[4, :, lanes]

        def outputs(i, states):
            for u in range(UNROLL):
                at = pl.ds(i * UNROLL + u, SUBLANES, stride=span)
                value = signal[at, :]
                states = tuple(a * s + value for a, s in zip(decay, states))
                terms = [w * s for w, s in zip(weight, states)]
                while len(terms) > 1:
                    terms = [sum(terms[k : k + 2][1:], terms[k]) for k in range(0, len(terms), 2)]
                result[at, :] = terms[0]
            return states

        lax.fori_loop(0, span // UNROLL, outputs, tuple(ends[m] for m in range(modes)))
        conv_ref[:, lanes] = result[...].astype(jnp.bfloat16)


def finish_kernel(n_weights, counts, order_ref, modes_ref, *refs):
    refs, seq = list(refs), len(counts)

    def take(count):
        taken = refs[:count]
        del refs[:count]
        return taken

    pair_hbm, query_hbm = take(2 * n_weights), take(n_weights)
    x_hbm = [take(count) for count in counts]
    outs, (state_ref,) = take(seq), take(1)
    x_buf, pair_buf, query_buf, prod, out, ends, conv_buf, x_sem, pair_sem, query_sem = take(10)
    rows = x_buf.shape[1]
    channels = conv_buf.shape[1]
    groups = prod.shape[0]
    first = 2 * pair_sem.shape[1] + (n_weights + 1) // 2
    x_copies = [token_copies(x_hbm[i], x_buf.at[i], x_sem.at[i]) for i in range(seq)]
    pair_copies = weight_copies(order_ref, pair_hbm, pair_buf, pair_sem)
    query_copies = weight_copies(order_ref, query_hbm, query_buf, query_sem)
    for copy in pair_copies + x_copies[0] + x_copies[1]:
        copy.start()
    for copy in pair_copies:
        copy.wait()
    for i in range(seq):
        for copy in x_copies[i]:
            copy.wait()
        for copy in x_copies[i + 2] if i + 2 < seq else query_copies if i + 2 == seq else ():
            copy.start()
        acc = jnp.dot(x_buf[i], pair_buf[...], preferred_element_type=jnp.float32)
        rounded = acc.astype(jnp.bfloat16).astype(jnp.float32)
        product = (rounded[:, :channels] * rounded[:, channels:]).astype(jnp.bfloat16)
        to = pl.ds(pl.multiple_of(order_ref[first + i] * rows, rows), rows)
        for g in range(groups):
            prod[g, to, :] = product[:, g * LANES : (g + 1) * LANES].astype(jnp.float32)
    modes_over_time(modes_ref, prod, out, ends, conv_buf, state_ref)
    for copy in query_copies:
        copy.wait()
    for i in range(seq):
        shard = order_ref[first + i]
        acc = jnp.dot(x_buf[i], query_buf[...], preferred_element_type=jnp.float32)
        query = acc.astype(jnp.bfloat16).astype(jnp.float32)
        conv = conv_buf[pl.ds(pl.multiple_of(shard * rows, rows), rows), :].astype(jnp.float32)
        gated = (query * conv).astype(jnp.bfloat16)
        for step in range(seq):

            @pl.when(order_ref[first + seq + i] == step)
            def _():
                outs[step][...] = gated


def finish(order, xs, pair, query, decay_rate, residue, carried):
    quarters, share, width = query[0].shape
    seq = len(xs)
    rows, depth = xs[0][0].shape[1:]
    length, modes = seq * rows, decay_rate.shape[1]
    scale = mode_scale(decay_rate)
    table = jnp.stack(
        [
            jnp.exp(-decay_rate),
            jnp.exp(-decay_rate * (length // SUBLANES)),
            residue * scale,
            carried / scale,
            scale,
        ]
    ).transpose(0, 2, 1)
    vmem, anywhere = pl.BlockSpec(memory_space=pltpu.VMEM), pl.BlockSpec(memory_space=pl.ANY)
    arrays = [*pair, *query, *sum(xs, [])]
    *gated, state = pl.pallas_call(
        functools.partial(finish_kernel, len(query), [len(x) for x in xs]),
        out_shape=tuple(jax.ShapeDtypeStruct((rows, width), jnp.bfloat16) for _ in range(seq))
        + (jax.ShapeDtypeStruct((modes, width), jnp.float32),),
        in_specs=[pl.BlockSpec(memory_space=pltpu.SMEM), vmem]
        + [anywhere] * len(arrays),
        out_specs=(vmem,) * (seq + 1),
        scratch_shapes=[
            pltpu.VMEM((seq, rows, quarters * depth), jnp.bfloat16),
            pltpu.VMEM((quarters * depth, 2 * width), jnp.bfloat16),
            pltpu.VMEM((quarters * depth, width), jnp.bfloat16),
            pltpu.VMEM((width // LANES, length, LANES), jnp.float32),
            pltpu.VMEM((width // LANES, length, LANES), jnp.float32),
            pltpu.VMEM((modes, SUBLANES, LANES), jnp.float32),
            pltpu.VMEM((length, width), jnp.bfloat16),
            pltpu.SemaphoreType.DMA((seq, quarters)),
            pltpu.SemaphoreType.DMA((len(pair) + 2 >> 1, quarters)),
            pltpu.SemaphoreType.DMA((len(query) + 1 >> 1, quarters)),
        ],
        compiler_params=pltpu.CompilerParams(vmem_limit_bytes=KERNEL_BYTES),
        cost_estimate=pl.CostEstimate(
            flops=FINISH_COST * length * quarters * depth * width,
            bytes_accessed=2 * quarters * depth * (length + 3 * width),
            transcendentals=0,
        ),
        name="finish",
    )(order, table, *arrays)
    return gated, state.T


def place_columns(pieces, place):
    seq = len(pieces)
    rows, width = pieces[0].shape

    def kernel(place_ref, *refs):
        out_ref = refs[-1]
        for step in range(seq):
            origin = place_ref[0] ^ step
            out_ref[:, pl.ds(pl.multiple_of(origin * width, width), width)] = refs[step][...]

    return pl.pallas_call(
        kernel,
        out_shape=jax.ShapeDtypeStruct((rows, seq * width), pieces[0].dtype),
        in_specs=[pl.BlockSpec(memory_space=pltpu.SMEM)] + [pl.BlockSpec(memory_space=pltpu.VMEM)] * seq,
        out_specs=pl.BlockSpec(memory_space=pltpu.VMEM),
        name="place_columns",
    )(place.reshape(1).astype(jnp.int32), *pieces)


def by_channels(sizes, tokens, w_query, w_key, w_value, decay_rate, residue, carried):
    seq, chan, rep, parts = sizes["seq"], sizes["chan"], sizes["rep"], sizes["parts"]
    place, x_place, core = lax.axis_index("seq"), lax.axis_index("chan"), lax.axis_index("rep")
    orders = arrival_order(seq)

    def at_place(choices):
        value = choices[0]
        for i in range(1, seq):
            value = jnp.where(place == i, choices[i], value)
        return value

    w_keys, w_values, w_queries = [exchange_weights(w, sizes) for w in (w_key, w_value, w_query)]
    before = {2: w_keys[:1], 3: w_keys[-1:] + w_values[:1], 4: w_values[-1:]}
    shares = [(lax.axis_index("parts") - turn) % parts for turn in range(parts)]
    features = [
        ((x_place - turn) % chan) * rep + (core - other) % rep for other in range(rep) for turn in range(chan)
    ]
    positions = [sum(jnp.where(f == place ^ step, q, 0) for q, f in enumerate(features)) for step in range(seq)]
    by_feature = jnp.stack([jnp.int32(i) for i in features + shares + positions])
    arrival, ways, xs, origins, last = tokens, [{0: tokens}, {0: tokens}], [], [place], None
    for phase in range(1, seq + 1):
        group = [arrival]
        for turn in range(1, chan):
            last = lax.ppermute(arrival, "chan", ring(chan, turn))
            group.append(last)
        if phase == seq:
            group[-1] = after(group[-1], w_queries[-1])
            group = [x[None] for x in group]
        else:
            group = [jnp.stack(group)]
        swapped = [lax.ppermute(x, "rep", ring(rep, turn)) for turn in range(1, rep) for x in group]
        xs.append(group + swapped)
        if phase == seq:
            break
        ups = [(i, i + 1) for i in range(phase - 1, seq - 1)]
        downs = [(i + 1, i) for i in range(seq - phase)]
        ways[0][phase] = lax.ppermute(ways[0][phase - 1], "seq", ups)
        ways[1][phase] = lax.ppermute(ways[1][phase - 1], "seq", downs)
        chosen = [orders[i][phase - 1] for i in range(seq)]
        sources = sorted({(way, step) for way, step, origin in chosen})
        index = at_place([jnp.int32(sources.index((way, step))) for way, step, origin in chosen])
        arrival = choose(
            index,
            [ways[way][step] for way, step in sources],
            [last, *before.get(phase + 1, ())],
            WEIGHT if phase == seq - 1 else 0,
        )
        origins.append(at_place([jnp.int32(origin) for way, step, origin in chosen]))

    steps = [place ^ origin for origin in origins]
    order = jnp.concatenate([by_feature, jnp.stack([jnp.int32(i) for i in origins + steps])])

    gated, new_state = finish(order, xs, w_keys + w_values, w_queries, decay_rate, residue, carried)
    pieces = [
        lax.ppermute(gated[step], "seq", mirror(seq, step)) if step else gated[0] for step in range(seq)
    ]
    return place_columns(pieces, place), new_state


def solution(mesh):
    in_specs = (
        P(("parts", "seq"), ("chan", "rep")),
        P("seq", ("chan", "rep")),
        P("seq", ("chan", "rep")),
        P("seq", ("chan", "rep")),
        P(("chan", "rep", "seq"), None),
        P(("chan", "rep", "seq"), None),
        P(("parts", "chan", "rep", "seq"), None),
    )
    out_specs = (P(("parts", "seq"), ("chan", "rep")), P(("parts", "chan", "rep", "seq"), None))
    sizes = dict(mesh.shape)

    def program(*arrays):
        tokens = arrays[0]
        part_bytes = tokens.size * tokens.dtype.itemsize * sizes["seq"] * sizes["chan"] * sizes["rep"]
        seq = sizes["seq"]
        fits = part_bytes <= GATHER_BYTES and seq == sizes["chan"] * sizes["rep"]
        fits = fits and seq >= 4 and seq & (seq - 1) == 0
        if fits:
            return by_channels(sizes, *arrays)
        return per_device(*arrays)

    return jax.shard_map(
        program, mesh=mesh, in_specs=in_specs, out_specs=out_specs, check_vma=False
    )
```

```python
import functools

import jax
import jax.numpy as jnp
from jax import lax
from jax.experimental import pallas as pl
from jax.experimental.pallas import tpu as pltpu
from jax.sharding import PartitionSpec as P

BLOCK = 128
SUBLANES, LANES = 8, 128
TILE = 256
UNROLL = 8
GATHER_BYTES = 24 << 20
KERNEL_BYTES = 56 << 20
FINISH_COST = 4
WEIGHT = 23 * 10**9


HIGHEST_PRECISION = lax.Precision.HIGHEST


def mode_scale(decay_rates):
    return jnp.sqrt(-jnp.expm1(-2.0 * decay_rates))


def local_ends(blocks, decay_rates):
    block_width = blocks.shape[2]
    offsets = jnp.arange(block_width, dtype=jnp.float32)
    tail_powers = jnp.exp(-decay_rates[:, :, None] * (block_width - 1.0 - offsets)[None, None, :])
    sums_here = jnp.einsum("cnb,cmb->cnm", blocks, tail_powers, precision=HIGHEST_PRECISION)
    return mode_scale(decay_rates)[:, None, :] * sums_here


def combine_states(earlier, later):
    return (earlier[0] * later[0], later[0] * earlier[1] + later[1])


def block_sums(block_ends, decay_rates, block_width):
    step_decay = jnp.broadcast_to(jnp.exp(-decay_rates * block_width)[:, None, :], block_ends.shape)
    unused_decay, running = lax.associative_scan(combine_states, (step_decay, block_ends), axis=1)
    return running


def entering_states(running, decay_rates, start_state, block_width):
    count_blocks = running.shape[1]
    block_starts = jnp.arange(count_blocks, dtype=jnp.float32) * block_width
    decayed = (
        jnp.exp(-decay_rates[:, None, :] * block_starts[None, :, None]) * start_state[:, None, :]
    )
    earlier_sums = jnp.concatenate([jnp.zeros_like(running[:, :1]), running[:, :-1]], axis=1)
    final_state = (
        jnp.exp(-decay_rates * (count_blocks * block_width)) * start_state + running[:, -1]
    )
    return (decayed + earlier_sums, final_state)


def block_convolve(blocks, decay_rates, residues, entering):
    block_width = blocks.shape[2]
    offsets = jnp.arange(block_width, dtype=jnp.float32)
    powers = jnp.exp(-decay_rates[:, :, None] * offsets[None, None, :])
    kernel = jnp.sum((residues * mode_scale(decay_rates))[:, :, None] * powers, axis=1)
    out_index = jnp.arange(block_width, dtype=jnp.int32)[:, None]
    in_index = jnp.arange(block_width, dtype=jnp.int32)[None, :]
    lag = jnp.maximum(out_index - in_index, 0)
    causal = (out_index >= in_index).astype(jnp.float32)
    toeplitz = kernel[:, lag] * causal[None, :, :]
    direct = jnp.einsum("cij,cnj->cni", toeplitz, blocks, precision=HIGHEST_PRECISION)
    leading = residues[:, :, None] * jnp.exp(
        -decay_rates[:, :, None] * (offsets + 1.0)[None, None, :]
    )
    return direct + jnp.einsum("cnm,cmb->cnb", entering, leading, precision=HIGHEST_PRECISION)


def per_device(tokens, w_query, w_key, w_value, decay_rate, residue, carried):
    gathered = lax.all_gather(tokens, ("chan", "rep"), axis=1, tiled=True)
    pieces = (
        lax.all_gather(w_query, "seq", axis=0, tiled=True),
        lax.all_gather(w_key, "seq", axis=0, tiled=True),
        lax.all_gather(w_value, "seq", axis=0, tiled=True),
    )
    query_acc, key_acc, value_acc = tuple(
        (
            lax.dot_general(
                weight_piece, gathered, (((0,), (1,)), ((), ())), preferred_element_type=jnp.float32
            )
            for weight_piece in pieces
        )
    )
    query_rows = query_acc.astype(jnp.bfloat16)
    key_rows = key_acc.astype(jnp.bfloat16)
    value_rows = value_acc.astype(jnp.bfloat16)
    query_rows, key_rows, value_rows = lax.optimization_barrier((query_rows, key_rows, value_rows))
    product = (key_rows.astype(jnp.float32) * value_rows.astype(jnp.float32)).astype(jnp.bfloat16)
    owned = lax.all_to_all(product, "seq", split_axis=0, concat_axis=1, tiled=True)
    own_chan = owned.shape[0]
    blocks = owned.astype(jnp.float32).reshape(own_chan, -1, BLOCK)
    block_end = local_ends(blocks, decay_rate)
    running = block_sums(block_end, decay_rate, BLOCK)
    entering, new_state = entering_states(running, decay_rate, carried, BLOCK)
    conv_out = (
        block_convolve(blocks, decay_rate, residue, entering)
        .reshape(own_chan, -1)
        .astype(jnp.bfloat16)
    )
    conv_back = lax.all_to_all(conv_out, "seq", split_axis=1, concat_axis=0, tiled=True)
    conv_back = lax.optimization_barrier(conv_back)
    gated_rows = (query_rows.astype(jnp.float32) * conv_back.astype(jnp.float32)).astype(
        jnp.bfloat16
    )
    return (gated_rows.T, new_state)


def ring(size, step):
    return [(i, (i + step) % size) for i in range(size)]


def mirror(size, step):
    return [(i, i ^ step) for i in range(size)]


def choose(index, candidates, waits, weight=0):
    shape = candidates[0]

    def kernel(index_ref, *refs):
        for i in range(len(candidates)):

            @pl.when(index_ref[0] == i)
            def _():
                refs[-1][...] = refs[i][...]

    vmem = pl.BlockSpec(memory_space=pltpu.VMEM)
    return pl.pallas_call(
        kernel,
        out_shape=jax.ShapeDtypeStruct(shape.shape, shape.dtype),
        in_specs=[pl.BlockSpec(memory_space=pltpu.SMEM)]
        + [vmem] * len(candidates)
        + [pl.BlockSpec(memory_space=pl.ANY)] * len(waits),
        out_specs=vmem,
        cost_estimate=pl.CostEstimate(flops=weight, bytes_accessed=2 * shape.size, transcendentals=0),
        name="choose",
    )(index.reshape(1).astype(jnp.int32), *candidates, *waits)


def after(x, *waits):
    def nothing(*refs):
        del refs

    anywhere = pl.BlockSpec(memory_space=pl.ANY)
    return pl.pallas_call(
        nothing,
        out_shape=jax.ShapeDtypeStruct(x.shape, x.dtype),
        in_specs=[anywhere] * (1 + len(waits)),
        out_specs=anywhere,
        input_output_aliases={0: 0},
        name="after",
    )(x, *waits)


def arrival_order(size):
    orders = []
    for i in range(size):
        order = []
        for step in range(1, size):
            if i - step >= 0:
                order.append((0, step, i - step))
            if i + step < size:
                order.append((1, step, i + step))
        orders.append(order)
    return orders


def exchange_weights(weight, sizes):
    seq, parts = sizes["seq"], sizes["parts"]
    place, part = lax.axis_index("seq"), lax.axis_index("parts")
    depth, width = weight.shape[0], weight.shape[1] // seq
    share = depth // parts
    mine = jnp.stack(
        [lax.dynamic_slice(weight, (part * share, i * width), (share, width)) for i in range(seq)]
    )
    mine = lax.all_to_all(mine, "seq", split_axis=0, concat_axis=0, tiled=True)
    fetched = jnp.concatenate(
        [lax.dynamic_slice(mine, (place ^ step, 0, 0), (1, share, width)) for step in range(1, seq)]
    )
    shares = [mine]
    for turn in range(1, parts):
        first = (part - turn) % parts * share
        own = lax.dynamic_slice(weight, (first, place * width), (share, width))
        shares += [own, lax.ppermute(fetched, "parts", ring(parts, turn))]
    return shares


def weight_copies(order_ref, w_hbm, w_buf, w_sem):
    quarters, share, width = w_hbm[0].shape
    parts = w_buf.shape[0] // (quarters * share)
    each = 2 * parts - 1
    copies = []

    def add(source, k, quarter, turn, index):
        row = quarter * (parts * share) + order_ref[quarters + turn] * share
        at = w_buf.at[pl.ds(pl.multiple_of(row, share), share), pl.ds(k * width, width)]
        copies.append(pltpu.make_async_copy(source, at, w_sem.at[k * parts + turn, index]))

    for k in range(len(w_hbm) // each):
        mine, *others = w_hbm[k * each : (k + 1) * each]
        for q in range(quarters):
            add(mine.at[order_ref[q]], k, q, 0, q)
        for turn in range(1, parts):
            own, fetched = others[2 * turn - 2 : 2 * turn]
            for step in range(quarters):
                source = fetched.at[step - 1] if step else own
                add(source, k, order_ref[quarters + parts + step], turn, step)
    return copies


def token_copies(x_hbm, x_buf, x_sem):
    some, rows, depth = x_hbm[0].shape
    return [
        pltpu.make_async_copy(
            x_hbm[e].at[f], x_buf.at[:, pl.ds((e * some + f) * depth, depth)], x_sem.at[e * some + f]
        )
        for e in range(len(x_hbm))
        for f in range(some)
    ]


def product_rows(x_buf, pair_buf, channels):
    acc = jnp.dot(x_buf[...], pair_buf[...], preferred_element_type=jnp.float32)
    rounded = acc.astype(jnp.bfloat16).astype(jnp.float32)
    return (rounded[:, :channels] * rounded[:, channels:]).astype(jnp.bfloat16)


def product_kernel(n_weights, each, order_ref, *refs):
    pair_hbm, x_hbm, (out_ref, x_buf, pair_buf, x_sem, pair_sem) = refs[:n_weights], refs[n_weights:-5], refs[-5:]
    count, rows, channels = out_ref.shape
    x_copies = [
        token_copies(x_hbm[i * each : (i + 1) * each], x_buf.at[i], x_sem.at[i]) for i in range(count)
    ]
    pair_copies = weight_copies(order_ref, pair_hbm, pair_buf, pair_sem)
    for copy in pair_copies + sum(x_copies[:2], []):
        copy.start()
    for copy in pair_copies:
        copy.wait()
    for i in range(count):
        for copy in x_copies[i]:
            copy.wait()
        for copy in x_copies[i + 2] if i + 2 < count else ():
            copy.start()
        out_ref[i] = product_rows(x_buf.at[i], pair_buf, channels)


def early_products(order, xs, pair):
    quarters, share, width = pair[0].shape
    rows, depth = xs[0][0].shape[1:]
    anywhere = pl.BlockSpec(memory_space=pl.ANY)
    arrays = [*pair, *sum(xs, [])]
    return pl.pallas_call(
        functools.partial(product_kernel, len(pair), len(xs[0])),
        out_shape=jax.ShapeDtypeStruct((len(xs), rows, width), jnp.bfloat16),
        in_specs=[pl.BlockSpec(memory_space=pltpu.SMEM)] + [anywhere] * len(arrays),
        out_specs=pl.BlockSpec(memory_space=pltpu.VMEM),
        scratch_shapes=[
            pltpu.VMEM((len(xs), rows, quarters * depth), jnp.bfloat16),
            pltpu.VMEM((quarters * depth, 2 * width), jnp.bfloat16),
            pltpu.SemaphoreType.DMA((len(xs), quarters)),
            pltpu.SemaphoreType.DMA((len(pair) + 2 >> 1, quarters)),
        ],
        compiler_params=pltpu.CompilerParams(vmem_limit_bytes=KERNEL_BYTES),
        cost_estimate=pl.CostEstimate(
            flops=len(xs) * rows * quarters * depth * width // 4,
            bytes_accessed=depth * rows,
            transcendentals=0,
        ),
        name="early_products",
    )(order, *arrays)


def modes_over_time(modes_ref, prod, out, ends, conv_ref, state_ref):
    groups, length, lane_width = prod.shape
    modes = modes_ref.shape[1]
    span = length // SUBLANES
    zero = jnp.zeros((SUBLANES, LANES), jnp.float32)
    for g in range(groups):
        lanes = pl.ds(g * LANES, LANES)
        signal, result = prod.at[g], out.at[g]
        decay = [jnp.broadcast_to(modes_ref[0, m : m + 1, lanes], (SUBLANES, LANES)) for m in range(modes)]
        weight = [jnp.broadcast_to(modes_ref[2, m : m + 1, lanes], (SUBLANES, LANES)) for m in range(modes)]

        def sums(i, states):
            for u in range(UNROLL):
                value = signal[pl.ds(i * UNROLL + u, SUBLANES, stride=span), :]
                states = tuple(a * s + value for a, s in zip(decay, states))
            return states

        states = lax.fori_loop(0, span // UNROLL, sums, (zero,) * modes)
        for m in range(modes):
            ends[m] = states[m]
        state = modes_ref[3, :, lanes]
        over_span = modes_ref[1, :, lanes]
        for b in range(SUBLANES):
            end = ends[:, b, :]
            ends[:, b, :] = state
            state = over_span * state + end
        state_ref[:, lanes] = state * modes_ref[4, :, lanes]

        def outputs(i, states):
            for u in range(UNROLL):
                at = pl.ds(i * UNROLL + u, SUBLANES, stride=span)
                value = signal[at, :]
                states = tuple(a * s + value for a, s in zip(decay, states))
                terms = [w * s for w, s in zip(weight, states)]
                while len(terms) > 1:
                    terms = [sum(terms[k : k + 2][1:], terms[k]) for k in range(0, len(terms), 2)]
                result[at, :] = terms[0]
            return states

        lax.fori_loop(0, span // UNROLL, outputs, tuple(ends[m] for m in range(modes)))
        conv_ref[:, lanes] = result[...].astype(jnp.bfloat16)


def finish_kernel(n_weights, counts, order_ref, modes_ref, *refs):
    refs, seq = list(refs), len(counts)

    def take(count):
        taken = refs[:count]
        del refs[:count]
        return taken

    (early_ref,) = take(1)
    pair_hbm, query_hbm = take(2 * n_weights), take(n_weights)
    x_hbm = [take(count) for count in counts]
    outs, (state_ref,) = take(seq), take(1)
    x_buf, pair_buf, query_buf, prod, out, ends, conv_buf, x_sem, pair_sem, query_sem = take(10)
    rows = x_buf.shape[1]
    channels = conv_buf.shape[1]
    groups = prod.shape[0]
    first = 2 * pair_sem.shape[1] + (n_weights + 1) // 2
    last = seq - 1
    x_copies = [token_copies(x_hbm[i], x_buf.at[i], x_sem.at[i]) for i in range(seq)]
    pair_copies = weight_copies(order_ref, pair_hbm, pair_buf, pair_sem)
    query_copies = weight_copies(order_ref, query_hbm, query_buf, query_sem)
    for copy in pair_copies + x_copies[last]:
        copy.start()

    def put(i, product):
        to = pl.ds(pl.multiple_of(order_ref[first + i] * rows, rows), rows)
        for g in range(groups):
            prod[g, to, :] = product[:, g * LANES : (g + 1) * LANES].astype(jnp.float32)

    for i in range(last):
        put(i, early_ref[i])
    for copy in pair_copies + x_copies[last]:
        copy.wait()
    for copy in query_copies + sum(x_copies[:last], []):
        copy.start()
    put(last, product_rows(x_buf.at[last], pair_buf, channels))
    modes_over_time(modes_ref, prod, out, ends, conv_buf, state_ref)
    for copy in query_copies + sum(x_copies[:last], []):
        copy.wait()
    for i in range(seq):
        shard = order_ref[first + i]
        acc = jnp.dot(x_buf[i], query_buf[...], preferred_element_type=jnp.float32)
        query = acc.astype(jnp.bfloat16).astype(jnp.float32)
        conv = conv_buf[pl.ds(pl.multiple_of(shard * rows, rows), rows), :].astype(jnp.float32)
        gated = (query * conv).astype(jnp.bfloat16)
        for step in range(seq):

            @pl.when(order_ref[first + seq + i] == step)
            def _():
                outs[step][...] = gated


def finish(order, early, xs, pair, query, decay_rate, residue, carried):
    quarters, share, width = query[0].shape
    seq = len(xs)
    rows, depth = xs[0][0].shape[1:]
    length, modes = seq * rows, decay_rate.shape[1]
    scale = mode_scale(decay_rate)
    table = jnp.stack(
        [
            jnp.exp(-decay_rate),
            jnp.exp(-decay_rate * (length // SUBLANES)),
            residue * scale,
            carried / scale,
            scale,
        ]
    ).transpose(0, 2, 1)
    vmem, anywhere = pl.BlockSpec(memory_space=pltpu.VMEM), pl.BlockSpec(memory_space=pl.ANY)
    arrays = [*pair, *query, *sum(xs, [])]
    *gated, state = pl.pallas_call(
        functools.partial(finish_kernel, len(query), [len(x) for x in xs]),
        out_shape=tuple(jax.ShapeDtypeStruct((rows, width), jnp.bfloat16) for _ in range(seq))
        + (jax.ShapeDtypeStruct((modes, width), jnp.float32),),
        in_specs=[pl.BlockSpec(memory_space=pltpu.SMEM), vmem, vmem]
        + [anywhere] * len(arrays),
        out_specs=(vmem,) * (seq + 1),
        scratch_shapes=[
            pltpu.VMEM((seq, rows, quarters * depth), jnp.bfloat16),
            pltpu.VMEM((quarters * depth, 2 * width), jnp.bfloat16),
            pltpu.VMEM((quarters * depth, width), jnp.bfloat16),
            pltpu.VMEM((width // LANES, length, LANES), jnp.float32),
            pltpu.VMEM((width // LANES, length, LANES), jnp.float32),
            pltpu.VMEM((modes, SUBLANES, LANES), jnp.float32),
            pltpu.VMEM((length, width), jnp.bfloat16),
            pltpu.SemaphoreType.DMA((seq, quarters)),
            pltpu.SemaphoreType.DMA((len(pair) + 2 >> 1, quarters)),
            pltpu.SemaphoreType.DMA((len(query) + 1 >> 1, quarters)),
        ],
        compiler_params=pltpu.CompilerParams(vmem_limit_bytes=KERNEL_BYTES),
        cost_estimate=pl.CostEstimate(
            flops=FINISH_COST * length * quarters * depth * width,
            bytes_accessed=2 * quarters * depth * (length + 3 * width),
            transcendentals=0,
        ),
        name="finish",
    )(order, table, early, *arrays)
    return gated, state.T


def place_columns(pieces, place):
    seq = len(pieces)
    rows, width = pieces[0].shape

    def kernel(place_ref, *refs):
        out_ref = refs[-1]
        for step in range(seq):
            origin = place_ref[0] ^ step
            out_ref[:, pl.ds(pl.multiple_of(origin * width, width), width)] = refs[step][...]

    return pl.pallas_call(
        kernel,
        out_shape=jax.ShapeDtypeStruct((rows, seq * width), pieces[0].dtype),
        in_specs=[pl.BlockSpec(memory_space=pltpu.SMEM)] + [pl.BlockSpec(memory_space=pltpu.VMEM)] * seq,
        out_specs=pl.BlockSpec(memory_space=pltpu.VMEM),
        name="place_columns",
    )(place.reshape(1).astype(jnp.int32), *pieces)


def by_channels(sizes, tokens, w_query, w_key, w_value, decay_rate, residue, carried):
    seq, chan, rep, parts = sizes["seq"], sizes["chan"], sizes["rep"], sizes["parts"]
    place, x_place, core = lax.axis_index("seq"), lax.axis_index("chan"), lax.axis_index("rep")
    orders = arrival_order(seq)

    def at_place(choices):
        value = choices[0]
        for i in range(1, seq):
            value = jnp.where(place == i, choices[i], value)
        return value

    w_keys, w_values, w_queries = [exchange_weights(w, sizes) for w in (w_key, w_value, w_query)]
    before = {2: w_keys[:1], 3: w_keys[-1:] + w_values[:1], 4: w_values[-1:]}
    shares = [(lax.axis_index("parts") - turn) % parts for turn in range(parts)]
    features = [
        ((x_place - turn) % chan) * rep + (core - other) % rep for other in range(rep) for turn in range(chan)
    ]
    positions = [sum(jnp.where(f == place ^ step, q, 0) for q, f in enumerate(features)) for step in range(seq)]
    by_feature = jnp.stack([jnp.int32(i) for i in features + shares + positions])
    arrival, ways, xs, origins, last = tokens, [{0: tokens}, {0: tokens}], [], [place], None
    for phase in range(1, seq + 1):
        group = [arrival]
        for turn in range(1, chan):
            last = lax.ppermute(arrival, "chan", ring(chan, turn))
            group.append(last)
        if phase == seq:
            early = early_products(by_feature, xs, w_keys + w_values)
            group[-1] = after(group[-1], early, w_queries[-1])
            group = [x[None] for x in group]
        else:
            group = [jnp.stack(group)]
        swapped = [lax.ppermute(x, "rep", ring(rep, turn)) for turn in range(1, rep) for x in group]
        xs.append(group + swapped)
        if phase == seq:
            break
        ups = [(i, i + 1) for i in range(phase - 1, seq - 1)]
        downs = [(i + 1, i) for i in range(seq - phase)]
        ways[0][phase] = lax.ppermute(ways[0][phase - 1], "seq", ups)
        ways[1][phase] = lax.ppermute(ways[1][phase - 1], "seq", downs)
        chosen = [orders[i][phase - 1] for i in range(seq)]
        sources = sorted({(way, step) for way, step, origin in chosen})
        index = at_place([jnp.int32(sources.index((way, step))) for way, step, origin in chosen])
        arrival = choose(
            index,
            [ways[way][step] for way, step in sources],
            [last, *before.get(phase + 1, ())],
            WEIGHT if phase == seq - 1 else 0,
        )
        origins.append(at_place([jnp.int32(origin) for way, step, origin in chosen]))

    steps = [place ^ origin for origin in origins]
    order = jnp.concatenate([by_feature, jnp.stack([jnp.int32(i) for i in origins + steps])])

    gated, new_state = finish(order, early, xs, w_keys + w_values, w_queries, decay_rate, residue, carried)
    pieces = [
        lax.ppermute(gated[step], "seq", mirror(seq, step)) if step else gated[0] for step in range(seq)
    ]
    return place_columns(pieces, place), new_state


def solution(mesh):
    in_specs = (
        P(("parts", "seq"), ("chan", "rep")),
        P("seq", ("chan", "rep")),
        P("seq", ("chan", "rep")),
        P("seq", ("chan", "rep")),
        P(("chan", "rep", "seq"), None),
        P(("chan", "rep", "seq"), None),
        P(("parts", "chan", "rep", "seq"), None),
    )
    out_specs = (P(("parts", "seq"), ("chan", "rep")), P(("parts", "chan", "rep", "seq"), None))
    sizes = dict(mesh.shape)

    def program(*arrays):
        tokens = arrays[0]
        part_bytes = tokens.size * tokens.dtype.itemsize * sizes["seq"] * sizes["chan"] * sizes["rep"]
        seq = sizes["seq"]
        fits = part_bytes <= GATHER_BYTES and seq == sizes["chan"] * sizes["rep"]
        fits = fits and seq >= 4 and seq & (seq - 1) == 0
        if fits:
            return by_channels(sizes, *arrays)
        return per_device(*arrays)

    return jax.shard_map(
        program, mesh=mesh, in_specs=in_specs, out_specs=out_specs, check_vma=False
    )
```

```python
import functools

import jax
import jax.numpy as jnp
from jax import lax
from jax.experimental import pallas as pl
from jax.experimental.pallas import tpu as pltpu
from jax.sharding import PartitionSpec as P

BLOCK = 128
SUBLANES, LANES = 8, 128
TILE = 256
UNROLL = 8
GATHER_BYTES = 24 << 20
KERNEL_BYTES = 56 << 20
FINISH_COST = 4
AHEAD = 2 * 10**9
WEIGHT = 23 * 10**9


HIGHEST_PRECISION = lax.Precision.HIGHEST


def mode_scale(decay_rates):
    return jnp.sqrt(-jnp.expm1(-2.0 * decay_rates))


def local_ends(blocks, decay_rates):
    block_width = blocks.shape[2]
    offsets = jnp.arange(block_width, dtype=jnp.float32)
    tail_powers = jnp.exp(-decay_rates[:, :, None] * (block_width - 1.0 - offsets)[None, None, :])
    sums_here = jnp.einsum("cnb,cmb->cnm", blocks, tail_powers, precision=HIGHEST_PRECISION)
    return mode_scale(decay_rates)[:, None, :] * sums_here


def combine_states(earlier, later):
    return (earlier[0] * later[0], later[0] * earlier[1] + later[1])


def block_sums(block_ends, decay_rates, block_width):
    step_decay = jnp.broadcast_to(jnp.exp(-decay_rates * block_width)[:, None, :], block_ends.shape)
    unused_decay, running = lax.associative_scan(combine_states, (step_decay, block_ends), axis=1)
    return running


def entering_states(running, decay_rates, start_state, block_width):
    count_blocks = running.shape[1]
    block_starts = jnp.arange(count_blocks, dtype=jnp.float32) * block_width
    decayed = (
        jnp.exp(-decay_rates[:, None, :] * block_starts[None, :, None]) * start_state[:, None, :]
    )
    earlier_sums = jnp.concatenate([jnp.zeros_like(running[:, :1]), running[:, :-1]], axis=1)
    final_state = (
        jnp.exp(-decay_rates * (count_blocks * block_width)) * start_state + running[:, -1]
    )
    return (decayed + earlier_sums, final_state)


def block_convolve(blocks, decay_rates, residues, entering):
    block_width = blocks.shape[2]
    offsets = jnp.arange(block_width, dtype=jnp.float32)
    powers = jnp.exp(-decay_rates[:, :, None] * offsets[None, None, :])
    kernel = jnp.sum((residues * mode_scale(decay_rates))[:, :, None] * powers, axis=1)
    out_index = jnp.arange(block_width, dtype=jnp.int32)[:, None]
    in_index = jnp.arange(block_width, dtype=jnp.int32)[None, :]
    lag = jnp.maximum(out_index - in_index, 0)
    causal = (out_index >= in_index).astype(jnp.float32)
    toeplitz = kernel[:, lag] * causal[None, :, :]
    direct = jnp.einsum("cij,cnj->cni", toeplitz, blocks, precision=HIGHEST_PRECISION)
    leading = residues[:, :, None] * jnp.exp(
        -decay_rates[:, :, None] * (offsets + 1.0)[None, None, :]
    )
    return direct + jnp.einsum("cnm,cmb->cnb", entering, leading, precision=HIGHEST_PRECISION)


def per_device(tokens, w_query, w_key, w_value, decay_rate, residue, carried):
    gathered = lax.all_gather(tokens, ("chan", "rep"), axis=1, tiled=True)
    pieces = (
        lax.all_gather(w_query, "seq", axis=0, tiled=True),
        lax.all_gather(w_key, "seq", axis=0, tiled=True),
        lax.all_gather(w_value, "seq", axis=0, tiled=True),
    )
    query_acc, key_acc, value_acc = tuple(
        (
            lax.dot_general(
                weight_piece, gathered, (((0,), (1,)), ((), ())), preferred_element_type=jnp.float32
            )
            for weight_piece in pieces
        )
    )
    query_rows = query_acc.astype(jnp.bfloat16)
    key_rows = key_acc.astype(jnp.bfloat16)
    value_rows = value_acc.astype(jnp.bfloat16)
    query_rows, key_rows, value_rows = lax.optimization_barrier((query_rows, key_rows, value_rows))
    product = (key_rows.astype(jnp.float32) * value_rows.astype(jnp.float32)).astype(jnp.bfloat16)
    owned = lax.all_to_all(product, "seq", split_axis=0, concat_axis=1, tiled=True)
    own_chan = owned.shape[0]
    blocks = owned.astype(jnp.float32).reshape(own_chan, -1, BLOCK)
    block_end = local_ends(blocks, decay_rate)
    running = block_sums(block_end, decay_rate, BLOCK)
    entering, new_state = entering_states(running, decay_rate, carried, BLOCK)
    conv_out = (
        block_convolve(blocks, decay_rate, residue, entering)
        .reshape(own_chan, -1)
        .astype(jnp.bfloat16)
    )
    conv_back = lax.all_to_all(conv_out, "seq", split_axis=1, concat_axis=0, tiled=True)
    conv_back = lax.optimization_barrier(conv_back)
    gated_rows = (query_rows.astype(jnp.float32) * conv_back.astype(jnp.float32)).astype(
        jnp.bfloat16
    )
    return (gated_rows.T, new_state)


def ring(size, step):
    return [(i, (i + step) % size) for i in range(size)]


def mirror(size, step):
    return [(i, i ^ step) for i in range(size)]


def choose(index, candidates, waits, weight=0):
    shape = candidates[0]

    def kernel(index_ref, *refs):
        for i in range(len(candidates)):

            @pl.when(index_ref[0] == i)
            def _():
                refs[-1][...] = refs[i][...]

    vmem = pl.BlockSpec(memory_space=pltpu.VMEM)
    return pl.pallas_call(
        kernel,
        out_shape=jax.ShapeDtypeStruct(shape.shape, shape.dtype),
        in_specs=[pl.BlockSpec(memory_space=pltpu.SMEM)]
        + [vmem] * len(candidates)
        + [pl.BlockSpec(memory_space=pl.ANY)] * len(waits),
        out_specs=vmem,
        cost_estimate=pl.CostEstimate(flops=weight, bytes_accessed=2 * shape.size, transcendentals=0),
        name="choose",
    )(index.reshape(1).astype(jnp.int32), *candidates, *waits)


def after(x, *waits, weight=0):
    def nothing(*refs):
        del refs

    anywhere = pl.BlockSpec(memory_space=pl.ANY)
    return pl.pallas_call(
        nothing,
        out_shape=jax.ShapeDtypeStruct(x.shape, x.dtype),
        in_specs=[anywhere] * (1 + len(waits)),
        out_specs=anywhere,
        input_output_aliases={0: 0},
        cost_estimate=pl.CostEstimate(flops=weight, bytes_accessed=weight // 300, transcendentals=0),
        name="after",
    )(x, *waits)


def arrival_order(size):
    orders = []
    for i in range(size):
        order = []
        for step in range(1, size):
            if i - step >= 0:
                order.append((0, step, i - step))
            if i + step < size:
                order.append((1, step, i + step))
        orders.append(order)
    return orders


def exchange_weights(weight, sizes):
    seq, parts = sizes["seq"], sizes["parts"]
    place, part = lax.axis_index("seq"), lax.axis_index("parts")
    depth, width = weight.shape[0], weight.shape[1] // seq
    share = depth // parts
    mine = jnp.stack(
        [lax.dynamic_slice(weight, (part * share, i * width), (share, width)) for i in range(seq)]
    )
    mine = lax.all_to_all(mine, "seq", split_axis=0, concat_axis=0, tiled=True)
    fetched = jnp.concatenate(
        [lax.dynamic_slice(mine, (place ^ step, 0, 0), (1, share, width)) for step in range(1, seq)]
    )
    shares = [mine]
    for turn in range(1, parts):
        first = (part - turn) % parts * share
        own = lax.dynamic_slice(weight, (first, place * width), (share, width))
        shares += [own, lax.ppermute(fetched, "parts", ring(parts, turn))]
    return shares


def weight_copies(order_ref, w_hbm, w_buf, w_sem):
    quarters, share, width = w_hbm[0].shape
    parts = w_buf.shape[0] // (quarters * share)
    each = 2 * parts - 1
    copies = []

    def add(source, k, quarter, turn, index):
        row = quarter * (parts * share) + order_ref[quarters + turn] * share
        at = w_buf.at[pl.ds(pl.multiple_of(row, share), share), pl.ds(k * width, width)]
        copies.append(pltpu.make_async_copy(source, at, w_sem.at[k * parts + turn, index]))

    for k in range(len(w_hbm) // each):
        mine, *others = w_hbm[k * each : (k + 1) * each]
        for q in range(quarters):
            add(mine.at[order_ref[q]], k, q, 0, q)
        for turn in range(1, parts):
            own, fetched = others[2 * turn - 2 : 2 * turn]
            for step in range(quarters):
                source = fetched.at[step - 1] if step else own
                add(source, k, order_ref[quarters + parts + step], turn, step)
    return copies


def token_copies(x_hbm, x_buf, x_sem):
    some, rows, depth = x_hbm[0].shape
    return [
        pltpu.make_async_copy(
            x_hbm[e].at[f], x_buf.at[:, pl.ds((e * some + f) * depth, depth)], x_sem.at[e * some + f]
        )
        for e in range(len(x_hbm))
        for f in range(some)
    ]


def product_rows(x_buf, pair_buf, channels):
    acc = jnp.dot(x_buf[...], pair_buf[...], preferred_element_type=jnp.float32)
    rounded = acc.astype(jnp.bfloat16).astype(jnp.float32)
    return (rounded[:, :channels] * rounded[:, channels:]).astype(jnp.bfloat16)


def product_kernel(n_weights, each, order_ref, *refs):
    pair_hbm, x_hbm, (out_ref, x_buf, pair_buf, x_sem, pair_sem) = refs[:n_weights], refs[n_weights:-5], refs[-5:]
    count, rows, channels = out_ref.shape
    x_copies = [
        token_copies(x_hbm[i * each : (i + 1) * each], x_buf.at[i], x_sem.at[i]) for i in range(count)
    ]
    pair_copies = weight_copies(order_ref, pair_hbm, pair_buf, pair_sem)
    for copy in pair_copies + sum(x_copies[:2], []):
        copy.start()
    for copy in pair_copies:
        copy.wait()
    for i in range(count):
        for copy in x_copies[i]:
            copy.wait()
        for copy in x_copies[i + 2] if i + 2 < count else ():
            copy.start()
        out_ref[i] = product_rows(x_buf.at[i], pair_buf, channels)


def early_products(order, xs, pair):
    quarters, share, width = pair[0].shape
    rows, depth = xs[0][0].shape[1:]
    anywhere = pl.BlockSpec(memory_space=pl.ANY)
    arrays = [*pair, *sum(xs, [])]
    return pl.pallas_call(
        functools.partial(product_kernel, len(pair), len(xs[0])),
        out_shape=jax.ShapeDtypeStruct((len(xs), rows, width), jnp.bfloat16),
        in_specs=[pl.BlockSpec(memory_space=pltpu.SMEM)] + [anywhere] * len(arrays),
        out_specs=pl.BlockSpec(memory_space=pltpu.VMEM),
        scratch_shapes=[
            pltpu.VMEM((len(xs), rows, quarters * depth), jnp.bfloat16),
            pltpu.VMEM((quarters * depth, 2 * width), jnp.bfloat16),
            pltpu.SemaphoreType.DMA((len(xs), quarters)),
            pltpu.SemaphoreType.DMA((len(pair) + 2 >> 1, quarters)),
        ],
        compiler_params=pltpu.CompilerParams(vmem_limit_bytes=KERNEL_BYTES),
        cost_estimate=pl.CostEstimate(
            flops=len(xs) * rows * quarters * depth * width // 4,
            bytes_accessed=depth * rows,
            transcendentals=0,
        ),
        name="early_products",
    )(order, *arrays)


def modes_over_time(modes_ref, prod, out, ends, conv_ref, state_ref):
    groups, length, lane_width = prod.shape
    modes = modes_ref.shape[1]
    span = length // SUBLANES
    zero = jnp.zeros((SUBLANES, LANES), jnp.float32)
    for g in range(groups):
        lanes = pl.ds(g * LANES, LANES)
        signal, result = prod.at[g], out.at[g]
        decay = [jnp.broadcast_to(modes_ref[0, m : m + 1, lanes], (SUBLANES, LANES)) for m in range(modes)]
        weight = [jnp.broadcast_to(modes_ref[2, m : m + 1, lanes], (SUBLANES, LANES)) for m in range(modes)]

        def sums(i, states):
            for u in range(UNROLL):
                value = signal[pl.ds(i * UNROLL + u, SUBLANES, stride=span), :]
                states = tuple(a * s + value for a, s in zip(decay, states))
            return states

        states = lax.fori_loop(0, span // UNROLL, sums, (zero,) * modes)
        for m in range(modes):
            ends[m] = states[m]
        state = modes_ref[3, :, lanes]
        over_span = modes_ref[1, :, lanes]
        for b in range(SUBLANES):
            end = ends[:, b, :]
            ends[:, b, :] = state
            state = over_span * state + end
        state_ref[:, lanes] = state * modes_ref[4, :, lanes]

        def outputs(i, states):
            for u in range(UNROLL):
                at = pl.ds(i * UNROLL + u, SUBLANES, stride=span)
                value = signal[at, :]
                states = tuple(a * s + value for a, s in zip(decay, states))
                terms = [w * s for w, s in zip(weight, states)]
                while len(terms) > 1:
                    terms = [sum(terms[k : k + 2][1:], terms[k]) for k in range(0, len(terms), 2)]
                result[at, :] = terms[0]
            return states

        lax.fori_loop(0, span // UNROLL, outputs, tuple(ends[m] for m in range(modes)))
        conv_ref[:, lanes] = result[...].astype(jnp.bfloat16)


def finish_kernel(n_weights, counts, order_ref, modes_ref, *refs):
    refs, seq = list(refs), len(counts)

    def take(count):
        taken = refs[:count]
        del refs[:count]
        return taken

    (early_ref,) = take(1)
    pair_hbm, query_hbm = take(2 * n_weights), take(n_weights)
    x_hbm = [take(count) for count in counts]
    outs, (conv_buf, state_ref) = take(seq - seq // 2), take(2)
    x_buf, pair_buf, query_buf, prod, out, ends, x_sem, pair_sem, query_sem = take(9)
    rows = x_buf.shape[1]
    channels = conv_buf.shape[1]
    groups = prod.shape[0]
    first = 2 * pair_sem.shape[1] + (n_weights + 1) // 2
    late = early_ref.shape[0]
    x_copies = [token_copies(x_hbm[i], x_buf.at[i], x_sem.at[i]) for i in range(seq)]
    pair_copies = weight_copies(order_ref, pair_hbm, pair_buf, pair_sem)
    query_copies = weight_copies(order_ref, query_hbm, query_buf, query_sem)
    for copy in pair_copies + sum(x_copies[late:], []):
        copy.start()

    def put(i, product):
        to = pl.ds(pl.multiple_of(order_ref[first + i] * rows, rows), rows)
        for g in range(groups):
            prod[g, to, :] = product[:, g * LANES : (g + 1) * LANES].astype(jnp.float32)

    for i in range(late):
        put(i, early_ref[i])
    for copy in pair_copies:
        copy.wait()
    for i in range(late, seq):
        for copy in x_copies[i]:
            copy.wait()
        if i == late:
            for copy in query_copies + sum(x_copies[:late], []):
                copy.start()
        put(i, product_rows(x_buf.at[i], pair_buf, channels))
    modes_over_time(modes_ref, prod, out, ends, conv_buf, state_ref)
    for copy in query_copies + sum(x_copies[:late], []):
        copy.wait()
    for step in range(seq // 2, seq):
        i = order_ref[first + 2 * seq + step]
        shard = order_ref[first + i]
        outs[step - seq // 2][...] = gated_rows(x_buf[i], query_buf, conv_buf, shard, rows)


def gated_rows(x, query_buf, conv_buf, shard, rows):
    acc = jnp.dot(x, query_buf[...], preferred_element_type=jnp.float32)
    query = acc.astype(jnp.bfloat16).astype(jnp.float32)
    conv = conv_buf[pl.ds(pl.multiple_of(shard * rows, rows), rows), :].astype(jnp.float32)
    return (query * conv).astype(jnp.bfloat16)


def near_kernel(n_weights, counts, order_ref, conv_ref, *refs):
    refs, seq = list(refs), len(counts)

    def take(count):
        taken = refs[:count]
        del refs[:count]
        return taken

    query_hbm = take(n_weights)
    x_hbm = [take(count) for count in counts]
    outs = take(seq // 2)
    x_buf, query_buf, x_sem, query_sem = take(4)
    rows = x_buf.shape[1]
    first = 2 * query_sem.shape[1] + (n_weights + 1) // 2
    query_copies = weight_copies(order_ref, query_hbm, query_buf, query_sem)
    x_copies = [token_copies(x_hbm[i], x_buf.at[i], x_sem.at[i]) for i in range(seq)]
    for copy in query_copies:
        copy.start()
    for i in range(seq):

        @pl.when(order_ref[first + seq + i] < seq // 2)
        def _():
            for copy in x_copies[i]:
                copy.start()

    for copy in query_copies:
        copy.wait()
    for i in range(seq):

        @pl.when(order_ref[first + seq + i] < seq // 2)
        def _():
            for copy in x_copies[i]:
                copy.wait()

    for step in range(seq // 2):
        i = order_ref[first + 2 * seq + step]
        outs[step][...] = gated_rows(x_buf[i], query_buf, conv_ref, order_ref[first + i], rows)


def gate_near(order, xs, query, conv):
    quarters, share, width = query[0].shape
    seq = len(xs)
    rows, depth = xs[0][0].shape[1:]
    vmem, anywhere = pl.BlockSpec(memory_space=pltpu.VMEM), pl.BlockSpec(memory_space=pl.ANY)
    arrays = [*query, *sum(xs, [])]
    return pl.pallas_call(
        functools.partial(near_kernel, len(query), [len(x) for x in xs]),
        out_shape=tuple(jax.ShapeDtypeStruct((rows, width), jnp.bfloat16) for _ in range(seq // 2)),
        in_specs=[pl.BlockSpec(memory_space=pltpu.SMEM), vmem] + [anywhere] * len(arrays),
        out_specs=(vmem,) * (seq // 2),
        scratch_shapes=[
            pltpu.VMEM((seq, rows, quarters * depth), jnp.bfloat16),
            pltpu.VMEM((quarters * depth, width), jnp.bfloat16),
            pltpu.SemaphoreType.DMA((seq, quarters)),
            pltpu.SemaphoreType.DMA((len(query) + 1 >> 1, quarters)),
        ],
        compiler_params=pltpu.CompilerParams(vmem_limit_bytes=KERNEL_BYTES),
        cost_estimate=pl.CostEstimate(
            flops=seq * rows * depth * quarters * width,
            bytes_accessed=quarters * depth * (seq * rows + 2 * width),
            transcendentals=0,
        ),
        name="gate_near",
    )(order, conv, *arrays)


def finish(order, early, xs, pair, query, decay_rate, residue, carried):
    quarters, share, width = query[0].shape
    seq = len(xs)
    rows, depth = xs[0][0].shape[1:]
    length, modes = seq * rows, decay_rate.shape[1]
    scale = mode_scale(decay_rate)
    table = jnp.stack(
        [
            jnp.exp(-decay_rate),
            jnp.exp(-decay_rate * (length // SUBLANES)),
            residue * scale,
            carried / scale,
            scale,
        ]
    ).transpose(0, 2, 1)
    vmem, anywhere = pl.BlockSpec(memory_space=pltpu.VMEM), pl.BlockSpec(memory_space=pl.ANY)
    arrays = [*pair, *query, *sum(xs, [])]
    *gated, conv, state = pl.pallas_call(
        functools.partial(finish_kernel, len(query), [len(x) for x in xs]),
        out_shape=tuple(jax.ShapeDtypeStruct((rows, width), jnp.bfloat16) for _ in range(seq - seq // 2))
        + (
            jax.ShapeDtypeStruct((length, width), jnp.bfloat16),
            jax.ShapeDtypeStruct((modes, width), jnp.float32),
        ),
        in_specs=[pl.BlockSpec(memory_space=pltpu.SMEM), vmem, vmem]
        + [anywhere] * len(arrays),
        out_specs=(vmem,) * (seq - seq // 2 + 2),
        scratch_shapes=[
            pltpu.VMEM((seq, rows, quarters * depth), jnp.bfloat16),
            pltpu.VMEM((quarters * depth, 2 * width), jnp.bfloat16),
            pltpu.VMEM((quarters * depth, width), jnp.bfloat16),
            pltpu.VMEM((width // LANES, length, LANES), jnp.float32),
            pltpu.VMEM((width // LANES, length, LANES), jnp.float32),
            pltpu.VMEM((modes, SUBLANES, LANES), jnp.float32),
            pltpu.SemaphoreType.DMA((seq, quarters)),
            pltpu.SemaphoreType.DMA((len(pair) + 2 >> 1, quarters)),
            pltpu.SemaphoreType.DMA((len(query) + 1 >> 1, quarters)),
        ],
        compiler_params=pltpu.CompilerParams(vmem_limit_bytes=KERNEL_BYTES),
        cost_estimate=pl.CostEstimate(
            flops=FINISH_COST * length * quarters * depth * width,
            bytes_accessed=2 * quarters * depth * (length + 3 * width),
            transcendentals=0,
        ),
        name="finish",
    )(order, table, early, *arrays)
    return gated, conv, state.T


def place_columns(pieces, place):
    seq = len(pieces)
    rows, width = pieces[0].shape

    def kernel(place_ref, *refs):
        out_ref = refs[-1]
        for step in range(seq):
            origin = place_ref[0] ^ step
            out_ref[:, pl.ds(pl.multiple_of(origin * width, width), width)] = refs[step][...]

    return pl.pallas_call(
        kernel,
        out_shape=jax.ShapeDtypeStruct((rows, seq * width), pieces[0].dtype),
        in_specs=[pl.BlockSpec(memory_space=pltpu.SMEM)] + [pl.BlockSpec(memory_space=pltpu.VMEM)] * seq,
        out_specs=pl.BlockSpec(memory_space=pltpu.VMEM),
        name="place_columns",
    )(place.reshape(1).astype(jnp.int32), *pieces)


def by_channels(sizes, tokens, w_query, w_key, w_value, decay_rate, residue, carried):
    seq, chan, rep, parts = sizes["seq"], sizes["chan"], sizes["rep"], sizes["parts"]
    place, x_place, core = lax.axis_index("seq"), lax.axis_index("chan"), lax.axis_index("rep")
    orders = arrival_order(seq)

    def at_place(choices):
        value = choices[0]
        for i in range(1, seq):
            value = jnp.where(place == i, choices[i], value)
        return value

    w_keys, w_values, w_queries = [exchange_weights(w, sizes) for w in (w_key, w_value, w_query)]
    before = {2: w_keys[:1], 3: w_keys[-1:] + w_values[:1], 4: w_values[-1:]}
    shares = [(lax.axis_index("parts") - turn) % parts for turn in range(parts)]
    features = [
        ((x_place - turn) % chan) * rep + (core - other) % rep for other in range(rep) for turn in range(chan)
    ]
    positions = [sum(jnp.where(f == place ^ step, q, 0) for q, f in enumerate(features)) for step in range(seq)]
    by_feature = jnp.stack([jnp.int32(i) for i in features + shares + positions])
    arrival, ways, xs, origins, last = tokens, [{0: tokens}, {0: tokens}], [], [place], None
    for phase in range(1, seq + 1):
        group = [arrival]
        for turn in range(1, chan):
            last = lax.ppermute(arrival, "chan", ring(chan, turn))
            group.append(last)
        if phase == seq:
            early = early_products(by_feature, xs[:-1], w_keys + w_values)
            group[-1] = after(group[-1], early, w_queries[-1])
            group = [x[None] for x in group]
        else:
            group = [jnp.stack(group)]
        swapped = [lax.ppermute(x, "rep", ring(rep, turn)) for turn in range(1, rep) for x in group]
        xs.append(group + swapped)
        if phase == seq:
            break
        ups = [(i, i + 1) for i in range(phase - 1, seq - 1)]
        downs = [(i + 1, i) for i in range(seq - phase)]
        ways[0][phase] = lax.ppermute(ways[0][phase - 1], "seq", ups)
        ways[1][phase] = lax.ppermute(ways[1][phase - 1], "seq", downs)
        chosen = [orders[i][phase - 1] for i in range(seq)]
        sources = sorted({(way, step) for way, step, origin in chosen})
        index = at_place([jnp.int32(sources.index((way, step))) for way, step, origin in chosen])
        arrival = choose(
            index,
            [ways[way][step] for way, step in sources],
            [last, *before.get(phase + 1, ())],
            WEIGHT if phase == seq - 1 else 0,
        )
        origins.append(at_place([jnp.int32(origin) for way, step, origin in chosen]))

    steps = [place ^ origin for origin in origins]
    by_step = [sum(jnp.where(near == step, i, 0) for i, near in enumerate(steps)) for step in range(seq)]
    order = jnp.concatenate([by_feature, jnp.stack([jnp.int32(i) for i in origins + steps + by_step])])

    far, conv, new_state = finish(order, early, xs, w_keys + w_values, w_queries, decay_rate, residue, carried)
    half = seq // 2
    pieces = {
        step: after(lax.ppermute(far[step - half], "seq", mirror(seq, step)), weight=AHEAD)
        for step in range(half, seq)
    }
    for step, piece in enumerate(gate_near(order, xs, w_queries, conv)):
        pieces[step] = lax.ppermute(piece, "seq", mirror(seq, step)) if step else piece
    pieces = [pieces[step] for step in range(seq)]
    return place_columns(pieces, place), new_state


def solution(mesh):
    in_specs = (
        P(("parts", "seq"), ("chan", "rep")),
        P("seq", ("chan", "rep")),
        P("seq", ("chan", "rep")),
        P("seq", ("chan", "rep")),
        P(("chan", "rep", "seq"), None),
        P(("chan", "rep", "seq"), None),
        P(("parts", "chan", "rep", "seq"), None),
    )
    out_specs = (P(("parts", "seq"), ("chan", "rep")), P(("parts", "chan", "rep", "seq"), None))
    sizes = dict(mesh.shape)

    def program(*arrays):
        tokens = arrays[0]
        part_bytes = tokens.size * tokens.dtype.itemsize * sizes["seq"] * sizes["chan"] * sizes["rep"]
        seq = sizes["seq"]
        fits = part_bytes <= GATHER_BYTES and seq == sizes["chan"] * sizes["rep"]
        fits = fits and seq >= 4 and seq & (seq - 1) == 0
        if fits:
            return by_channels(sizes, *arrays)
        return per_device(*arrays)

    return jax.shard_map(
        program, mesh=mesh, in_specs=in_specs, out_specs=out_specs, check_vma=False
    )
```

```python
import functools

import jax
import jax.numpy as jnp
from jax import lax
from jax.experimental import pallas as pl
from jax.experimental.pallas import tpu as pltpu
from jax.sharding import PartitionSpec as P

BLOCK = 128
SUBLANES, LANES = 8, 128
TILE = 256
UNROLL = 8
GATHER_BYTES = 24 << 20
KERNEL_BYTES = 56 << 20
FINISH_COST = 4
AHEAD = 2 * 10**9
WEIGHT = 23 * 10**9


HIGHEST_PRECISION = lax.Precision.HIGHEST


def mode_scale(decay_rates):
    return jnp.sqrt(-jnp.expm1(-2.0 * decay_rates))


def local_ends(blocks, decay_rates):
    block_width = blocks.shape[2]
    offsets = jnp.arange(block_width, dtype=jnp.float32)
    tail_powers = jnp.exp(-decay_rates[:, :, None] * (block_width - 1.0 - offsets)[None, None, :])
    sums_here = jnp.einsum("cnb,cmb->cnm", blocks, tail_powers, precision=HIGHEST_PRECISION)
    return mode_scale(decay_rates)[:, None, :] * sums_here


def combine_states(earlier, later):
    return (earlier[0] * later[0], later[0] * earlier[1] + later[1])


def block_sums(block_ends, decay_rates, block_width):
    step_decay = jnp.broadcast_to(jnp.exp(-decay_rates * block_width)[:, None, :], block_ends.shape)
    unused_decay, running = lax.associative_scan(combine_states, (step_decay, block_ends), axis=1)
    return running


def entering_states(running, decay_rates, start_state, block_width):
    count_blocks = running.shape[1]
    block_starts = jnp.arange(count_blocks, dtype=jnp.float32) * block_width
    decayed = (
        jnp.exp(-decay_rates[:, None, :] * block_starts[None, :, None]) * start_state[:, None, :]
    )
    earlier_sums = jnp.concatenate([jnp.zeros_like(running[:, :1]), running[:, :-1]], axis=1)
    final_state = (
        jnp.exp(-decay_rates * (count_blocks * block_width)) * start_state + running[:, -1]
    )
    return (decayed + earlier_sums, final_state)


def block_convolve(blocks, decay_rates, residues, entering):
    block_width = blocks.shape[2]
    offsets = jnp.arange(block_width, dtype=jnp.float32)
    powers = jnp.exp(-decay_rates[:, :, None] * offsets[None, None, :])
    kernel = jnp.sum((residues * mode_scale(decay_rates))[:, :, None] * powers, axis=1)
    out_index = jnp.arange(block_width, dtype=jnp.int32)[:, None]
    in_index = jnp.arange(block_width, dtype=jnp.int32)[None, :]
    lag = jnp.maximum(out_index - in_index, 0)
    causal = (out_index >= in_index).astype(jnp.float32)
    toeplitz = kernel[:, lag] * causal[None, :, :]
    direct = jnp.einsum("cij,cnj->cni", toeplitz, blocks, precision=HIGHEST_PRECISION)
    leading = residues[:, :, None] * jnp.exp(
        -decay_rates[:, :, None] * (offsets + 1.0)[None, None, :]
    )
    return direct + jnp.einsum("cnm,cmb->cnb", entering, leading, precision=HIGHEST_PRECISION)


def per_device(tokens, w_query, w_key, w_value, decay_rate, residue, carried):
    gathered = lax.all_gather(tokens, ("chan", "rep"), axis=1, tiled=True)
    pieces = (
        lax.all_gather(w_query, "seq", axis=0, tiled=True),
        lax.all_gather(w_key, "seq", axis=0, tiled=True),
        lax.all_gather(w_value, "seq", axis=0, tiled=True),
    )
    query_acc, key_acc, value_acc = tuple(
        (
            lax.dot_general(
                weight_piece, gathered, (((0,), (1,)), ((), ())), preferred_element_type=jnp.float32
            )
            for weight_piece in pieces
        )
    )
    query_rows = query_acc.astype(jnp.bfloat16)
    key_rows = key_acc.astype(jnp.bfloat16)
    value_rows = value_acc.astype(jnp.bfloat16)
    query_rows, key_rows, value_rows = lax.optimization_barrier((query_rows, key_rows, value_rows))
    product = (key_rows.astype(jnp.float32) * value_rows.astype(jnp.float32)).astype(jnp.bfloat16)
    owned = lax.all_to_all(product, "seq", split_axis=0, concat_axis=1, tiled=True)
    own_chan = owned.shape[0]
    blocks = owned.astype(jnp.float32).reshape(own_chan, -1, BLOCK)
    block_end = local_ends(blocks, decay_rate)
    running = block_sums(block_end, decay_rate, BLOCK)
    entering, new_state = entering_states(running, decay_rate, carried, BLOCK)
    conv_out = (
        block_convolve(blocks, decay_rate, residue, entering)
        .reshape(own_chan, -1)
        .astype(jnp.bfloat16)
    )
    conv_back = lax.all_to_all(conv_out, "seq", split_axis=1, concat_axis=0, tiled=True)
    conv_back = lax.optimization_barrier(conv_back)
    gated_rows = (query_rows.astype(jnp.float32) * conv_back.astype(jnp.float32)).astype(
        jnp.bfloat16
    )
    return (gated_rows.T, new_state)


def ring(size, step):
    return [(i, (i + step) % size) for i in range(size)]


def mirror(size, step):
    return [(i, i ^ step) for i in range(size)]


def choose(index, candidates, waits, weight=0):
    shape = candidates[0]

    def kernel(index_ref, *refs):
        for i in range(len(candidates)):

            @pl.when(index_ref[0] == i)
            def _():
                refs[-1][...] = refs[i][...]

    vmem = pl.BlockSpec(memory_space=pltpu.VMEM)
    return pl.pallas_call(
        kernel,
        out_shape=jax.ShapeDtypeStruct(shape.shape, shape.dtype),
        in_specs=[pl.BlockSpec(memory_space=pltpu.SMEM)]
        + [vmem] * len(candidates)
        + [pl.BlockSpec(memory_space=pl.ANY)] * len(waits),
        out_specs=vmem,
        cost_estimate=pl.CostEstimate(flops=weight, bytes_accessed=2 * shape.size, transcendentals=0),
        name="choose",
    )(index.reshape(1).astype(jnp.int32), *candidates, *waits)


def after(x, *waits, weight=0):
    def nothing(*refs):
        del refs

    anywhere = pl.BlockSpec(memory_space=pl.ANY)
    return pl.pallas_call(
        nothing,
        out_shape=jax.ShapeDtypeStruct(x.shape, x.dtype),
        in_specs=[anywhere] * (1 + len(waits)),
        out_specs=anywhere,
        input_output_aliases={0: 0},
        cost_estimate=pl.CostEstimate(flops=weight, bytes_accessed=weight // 300, transcendentals=0),
        name="after",
    )(x, *waits)


def arrival_order(size):
    orders = []
    for i in range(size):
        order = []
        for step in range(1, size):
            if i - step >= 0:
                order.append((0, step, i - step))
            if i + step < size:
                order.append((1, step, i + step))
        orders.append(order)
    return orders


def exchange_weights(weight, sizes):
    seq, parts = sizes["seq"], sizes["parts"]
    place, part = lax.axis_index("seq"), lax.axis_index("parts")
    depth, width = weight.shape[0], weight.shape[1] // seq
    share = depth // parts
    mine = jnp.stack(
        [lax.dynamic_slice(weight, (part * share, i * width), (share, width)) for i in range(seq)]
    )
    mine = lax.all_to_all(mine, "seq", split_axis=0, concat_axis=0, tiled=True)
    fetched = jnp.concatenate(
        [lax.dynamic_slice(mine, (place ^ step, 0, 0), (1, share, width)) for step in range(1, seq)]
    )
    shares = [mine]
    for turn in range(1, parts):
        first = (part - turn) % parts * share
        own = lax.dynamic_slice(weight, (first, place * width), (share, width))
        shares += [own, lax.ppermute(fetched, "parts", ring(parts, turn))]
    return shares


def weight_copies(order_ref, w_hbm, w_buf, w_sem):
    quarters, share, width = w_hbm[0].shape
    parts = w_buf.shape[0] // (quarters * share)
    each = 2 * parts - 1
    copies = []

    def add(source, k, quarter, turn, index):
        row = quarter * (parts * share) + order_ref[quarters + turn] * share
        at = w_buf.at[pl.ds(pl.multiple_of(row, share), share), pl.ds(k * width, width)]
        copies.append(pltpu.make_async_copy(source, at, w_sem.at[k * parts + turn, index]))

    for k in range(len(w_hbm) // each):
        mine, *others = w_hbm[k * each : (k + 1) * each]
        for q in range(quarters):
            add(mine.at[order_ref[q]], k, q, 0, q)
        for turn in range(1, parts):
            own, fetched = others[2 * turn - 2 : 2 * turn]
            for step in range(quarters):
                source = fetched.at[step - 1] if step else own
                add(source, k, order_ref[quarters + parts + step], turn, step)
    return copies


def token_copies(x_hbm, x_buf, x_sem):
    some, rows, depth = x_hbm[0].shape
    return [
        pltpu.make_async_copy(
            x_hbm[e].at[f], x_buf.at[:, pl.ds((e * some + f) * depth, depth)], x_sem.at[e * some + f]
        )
        for e in range(len(x_hbm))
        for f in range(some)
    ]


def product_rows(x_buf, pair_buf, channels):
    acc = jnp.dot(x_buf[...], pair_buf[...], preferred_element_type=jnp.float32)
    rounded = acc.astype(jnp.bfloat16).astype(jnp.float32)
    return (rounded[:, :channels] * rounded[:, channels:]).astype(jnp.bfloat16)


def product_kernel(n_weights, each, order_ref, *refs):
    pair_hbm, x_hbm, (out_ref, x_buf, pair_buf, x_sem, pair_sem) = refs[:n_weights], refs[n_weights:-5], refs[-5:]
    count, rows, channels = out_ref.shape
    x_copies = [
        token_copies(x_hbm[i * each : (i + 1) * each], x_buf.at[i], x_sem.at[i]) for i in range(count)
    ]
    pair_copies = weight_copies(order_ref, pair_hbm, pair_buf, pair_sem)
    for copy in pair_copies + sum(x_copies[:2], []):
        copy.start()
    for copy in pair_copies:
        copy.wait()
    for i in range(count):
        for copy in x_copies[i]:
            copy.wait()
        for copy in x_copies[i + 2] if i + 2 < count else ():
            copy.start()
        out_ref[i] = product_rows(x_buf.at[i], pair_buf, channels)


def early_products(order, xs, pair):
    quarters, share, width = pair[0].shape
    rows, depth = xs[0][0].shape[1:]
    anywhere = pl.BlockSpec(memory_space=pl.ANY)
    arrays = [*pair, *sum(xs, [])]
    return pl.pallas_call(
        functools.partial(product_kernel, len(pair), len(xs[0])),
        out_shape=jax.ShapeDtypeStruct((len(xs), rows, width), jnp.bfloat16),
        in_specs=[pl.BlockSpec(memory_space=pltpu.SMEM)] + [anywhere] * len(arrays),
        out_specs=pl.BlockSpec(memory_space=pltpu.VMEM),
        scratch_shapes=[
            pltpu.VMEM((len(xs), rows, quarters * depth), jnp.bfloat16),
            pltpu.VMEM((quarters * depth, 2 * width), jnp.bfloat16),
            pltpu.SemaphoreType.DMA((len(xs), quarters)),
            pltpu.SemaphoreType.DMA((len(pair) + 2 >> 1, quarters)),
        ],
        compiler_params=pltpu.CompilerParams(vmem_limit_bytes=KERNEL_BYTES),
        cost_estimate=pl.CostEstimate(
            flops=len(xs) * rows * quarters * depth * width // 4,
            bytes_accessed=depth * rows,
            transcendentals=0,
        ),
        name="early_products",
    )(order, *arrays)


def modes_over_time(modes_ref, prod, out, ends, conv_ref, state_ref):
    groups, length, lane_width = prod.shape
    modes = modes_ref.shape[1]
    span = length // SUBLANES
    zero = jnp.zeros((SUBLANES, LANES), jnp.float32)
    for g in range(groups):
        lanes = pl.ds(g * LANES, LANES)
        signal, result = prod.at[g], out.at[g]
        decay = [jnp.broadcast_to(modes_ref[0, m : m + 1, lanes], (SUBLANES, LANES)) for m in range(modes)]
        weight = [jnp.broadcast_to(modes_ref[2, m : m + 1, lanes], (SUBLANES, LANES)) for m in range(modes)]

        def sums(i, states):
            for u in range(UNROLL):
                value = signal[pl.ds(i * UNROLL + u, SUBLANES, stride=span), :]
                states = tuple(a * s + value for a, s in zip(decay, states))
            return states

        states = lax.fori_loop(0, span // UNROLL, sums, (zero,) * modes)
        for m in range(modes):
            ends[m] = states[m]
        state = modes_ref[3, :, lanes]
        over_span = modes_ref[1, :, lanes]
        for b in range(SUBLANES):
            end = ends[:, b, :]
            ends[:, b, :] = state
            state = over_span * state + end
        state_ref[:, lanes] = state * modes_ref[4, :, lanes]

        def outputs(i, states):
            for u in range(UNROLL):
                at = pl.ds(i * UNROLL + u, SUBLANES, stride=span)
                value = signal[at, :]
                states = tuple(a * s + value for a, s in zip(decay, states))
                terms = [w * s for w, s in zip(weight, states)]
                while len(terms) > 1:
                    terms = [sum(terms[k : k + 2][1:], terms[k]) for k in range(0, len(terms), 2)]
                result[at, :] = terms[0]
            return states

        lax.fori_loop(0, span // UNROLL, outputs, tuple(ends[m] for m in range(modes)))
        conv_ref[:, lanes] = result[...].astype(jnp.bfloat16)


def finish_kernel(n_weights, counts, order_ref, modes_ref, *refs):
    refs, seq = list(refs), len(counts)

    def take(count):
        taken = refs[:count]
        del refs[:count]
        return taken

    (early_ref,) = take(1)
    pair_hbm, query_hbm = take(2 * n_weights), take(n_weights)
    x_hbm = [take(count) for count in counts]
    outs, (conv_buf, state_ref) = take(seq - seq // 2), take(2)
    x_buf, pair_buf, query_buf, prod, out, ends, x_sem, pair_sem, query_sem = take(9)
    rows = x_buf.shape[1]
    channels = conv_buf.shape[1]
    groups = prod.shape[0]
    first = 2 * pair_sem.shape[1] + (n_weights + 1) // 2
    late = early_ref.shape[0]
    x_copies = [token_copies(x_hbm[i], x_buf.at[i], x_sem.at[i]) for i in range(seq)]
    pair_copies = weight_copies(order_ref, pair_hbm, pair_buf, pair_sem)
    query_copies = weight_copies(order_ref, query_hbm, query_buf, query_sem)
    for copy in pair_copies + sum(x_copies[late:], []):
        copy.start()

    def put(i, product):
        to = pl.ds(pl.multiple_of(order_ref[first + i] * rows, rows), rows)
        for g in range(groups):
            prod[g, to, :] = product[:, g * LANES : (g + 1) * LANES].astype(jnp.float32)

    for i in range(late):
        put(i, early_ref[i])
    for copy in pair_copies:
        copy.wait()
    for i in range(late, seq):
        for copy in x_copies[i]:
            copy.wait()
        if i == late:
            for copy in query_copies + sum(x_copies[:late], []):
                copy.start()
        put(i, product_rows(x_buf.at[i], pair_buf, channels))
    modes_over_time(modes_ref, prod, out, ends, conv_buf, state_ref)
    for copy in query_copies + sum(x_copies[:late], []):
        copy.wait()
    for step in range(seq // 2, seq):
        i = order_ref[first + 2 * seq + step]
        shard = order_ref[first + i]
        outs[step - seq // 2][...] = gated_rows(x_buf[i], query_buf, conv_buf, shard, rows)


def gated_rows(x, query_buf, conv_buf, shard, rows):
    acc = jnp.dot(x, query_buf[...], preferred_element_type=jnp.float32)
    query = acc.astype(jnp.bfloat16).astype(jnp.float32)
    conv = conv_buf[pl.ds(pl.multiple_of(shard * rows, rows), rows), :].astype(jnp.float32)
    return (query * conv).astype(jnp.bfloat16)


def near_kernel(n_weights, counts, order_ref, conv_ref, *refs):
    refs, seq = list(refs), len(counts)

    def take(count):
        taken = refs[:count]
        del refs[:count]
        return taken

    query_hbm = take(n_weights)
    x_hbm = [take(count) for count in counts]
    outs = take(seq // 2)
    x_buf, query_buf, x_sem, query_sem = take(4)
    rows = x_buf.shape[1]
    first = 2 * query_sem.shape[1] + (n_weights + 1) // 2
    query_copies = weight_copies(order_ref, query_hbm, query_buf, query_sem)
    x_copies = [token_copies(x_hbm[i], x_buf.at[i], x_sem.at[i]) for i in range(seq)]
    for copy in query_copies:
        copy.start()
    for i in range(seq):

        @pl.when(order_ref[first + seq + i] < seq // 2)
        def _():
            for copy in x_copies[i]:
                copy.start()

    for copy in query_copies:
        copy.wait()
    for i in range(seq):

        @pl.when(order_ref[first + seq + i] < seq // 2)
        def _():
            for copy in x_copies[i]:
                copy.wait()

    for step in range(seq // 2):
        i = order_ref[first + 2 * seq + step]
        outs[step][...] = gated_rows(x_buf[i], query_buf, conv_ref, order_ref[first + i], rows)


def gate_near(order, xs, query, conv):
    quarters, share, width = query[0].shape
    seq = len(xs)
    rows, depth = xs[0][0].shape[1:]
    vmem, anywhere = pl.BlockSpec(memory_space=pltpu.VMEM), pl.BlockSpec(memory_space=pl.ANY)
    arrays = [*query, *sum(xs, [])]
    return pl.pallas_call(
        functools.partial(near_kernel, len(query), [len(x) for x in xs]),
        out_shape=tuple(jax.ShapeDtypeStruct((rows, width), jnp.bfloat16) for _ in range(seq // 2)),
        in_specs=[pl.BlockSpec(memory_space=pltpu.SMEM), vmem] + [anywhere] * len(arrays),
        out_specs=(vmem,) * (seq // 2),
        scratch_shapes=[
            pltpu.VMEM((seq, rows, quarters * depth), jnp.bfloat16),
            pltpu.VMEM((quarters * depth, width), jnp.bfloat16),
            pltpu.SemaphoreType.DMA((seq, quarters)),
            pltpu.SemaphoreType.DMA((len(query) + 1 >> 1, quarters)),
        ],
        compiler_params=pltpu.CompilerParams(vmem_limit_bytes=KERNEL_BYTES),
        cost_estimate=pl.CostEstimate(
            flops=seq * rows * depth * quarters * width,
            bytes_accessed=quarters * depth * (seq * rows + 2 * width),
            transcendentals=0,
        ),
        name="gate_near",
    )(order, conv, *arrays)


def finish(order, early, xs, pair, query, decay_rate, residue, carried):
    quarters, share, width = query[0].shape
    seq = len(xs)
    rows, depth = xs[0][0].shape[1:]
    length, modes = seq * rows, decay_rate.shape[1]
    scale = mode_scale(decay_rate)
    table = jnp.stack(
        [
            jnp.exp(-decay_rate),
            jnp.exp(-decay_rate * (length // SUBLANES)),
            residue * scale,
            carried / scale,
            scale,
        ]
    ).transpose(0, 2, 1)
    vmem, anywhere = pl.BlockSpec(memory_space=pltpu.VMEM), pl.BlockSpec(memory_space=pl.ANY)
    arrays = [*pair, *query, *sum(xs, [])]
    *gated, conv, state = pl.pallas_call(
        functools.partial(finish_kernel, len(query), [len(x) for x in xs]),
        out_shape=tuple(jax.ShapeDtypeStruct((rows, width), jnp.bfloat16) for _ in range(seq - seq // 2))
        + (
            jax.ShapeDtypeStruct((length, width), jnp.bfloat16),
            jax.ShapeDtypeStruct((modes, width), jnp.float32),
        ),
        in_specs=[pl.BlockSpec(memory_space=pltpu.SMEM), vmem, vmem]
        + [anywhere] * len(arrays),
        out_specs=(vmem,) * (seq - seq // 2 + 2),
        scratch_shapes=[
            pltpu.VMEM((seq, rows, quarters * depth), jnp.bfloat16),
            pltpu.VMEM((quarters * depth, 2 * width), jnp.bfloat16),
            pltpu.VMEM((quarters * depth, width), jnp.bfloat16),
            pltpu.VMEM((width // LANES, length, LANES), jnp.float32),
            pltpu.VMEM((width // LANES, length, LANES), jnp.float32),
            pltpu.VMEM((modes, SUBLANES, LANES), jnp.float32),
            pltpu.SemaphoreType.DMA((seq, quarters)),
            pltpu.SemaphoreType.DMA((len(pair) + 2 >> 1, quarters)),
            pltpu.SemaphoreType.DMA((len(query) + 1 >> 1, quarters)),
        ],
        compiler_params=pltpu.CompilerParams(vmem_limit_bytes=KERNEL_BYTES),
        cost_estimate=pl.CostEstimate(
            flops=FINISH_COST * length * quarters * depth * width,
            bytes_accessed=2 * quarters * depth * (length + 3 * width),
            transcendentals=0,
        ),
        name="finish",
    )(order, table, early, *arrays)
    return gated, conv, state.T


def place_columns(pieces, place):
    seq = len(pieces)
    rows, width = pieces[0].shape

    def kernel(place_ref, *refs):
        out_ref = refs[-1]
        for step in range(seq):
            origin = place_ref[0] ^ step
            out_ref[:, pl.ds(pl.multiple_of(origin * width, width), width)] = refs[step][...]

    return pl.pallas_call(
        kernel,
        out_shape=jax.ShapeDtypeStruct((rows, seq * width), pieces[0].dtype),
        in_specs=[pl.BlockSpec(memory_space=pltpu.SMEM)] + [pl.BlockSpec(memory_space=pltpu.VMEM)] * seq,
        out_specs=pl.BlockSpec(memory_space=pltpu.VMEM),
        name="place_columns",
    )(place.reshape(1).astype(jnp.int32), *pieces)


def by_channels(sizes, tokens, w_query, w_key, w_value, decay_rate, residue, carried):
    seq, chan, rep, parts = sizes["seq"], sizes["chan"], sizes["rep"], sizes["parts"]
    place, x_place, core = lax.axis_index("seq"), lax.axis_index("chan"), lax.axis_index("rep")
    orders = arrival_order(seq)

    def at_place(choices):
        value = choices[0]
        for i in range(1, seq):
            value = jnp.where(place == i, choices[i], value)
        return value

    w_keys, w_values, w_queries = [exchange_weights(w, sizes) for w in (w_key, w_value, w_query)]
    before = {2: w_keys[:1], 3: w_keys[-1:] + w_values[:1], 4: w_values[-1:]}
    shares = [(lax.axis_index("parts") - turn) % parts for turn in range(parts)]
    features = [
        ((x_place - turn) % chan) * rep + (core - other) % rep for other in range(rep) for turn in range(chan)
    ]
    positions = [sum(jnp.where(f == place ^ step, q, 0) for q, f in enumerate(features)) for step in range(seq)]
    by_feature = jnp.stack([jnp.int32(i) for i in features + shares + positions])
    arrival, ways, xs, origins, last = tokens, [{0: tokens}, {0: tokens}], [], [place], None
    for phase in range(1, seq + 1):
        group = [arrival]
        for turn in range(1, chan):
            last = lax.ppermute(arrival, "chan", ring(chan, turn))
            group.append(last)
        if phase == seq:
            early = early_products(by_feature, xs[:-1], w_keys + w_values)
            group[-1] = after(group[-1], early, w_queries[-1])
        if phase >= seq - 1:
            group = [x[None] for x in group]
        else:
            group = [jnp.stack(group)]
        swapped = [lax.ppermute(x, "rep", ring(rep, turn)) for turn in range(1, rep) for x in group]
        xs.append(group + swapped)
        if phase == seq:
            break
        ups = [(i, i + 1) for i in range(phase - 1, seq - 1)]
        downs = [(i + 1, i) for i in range(seq - phase)]
        ways[0][phase] = lax.ppermute(ways[0][phase - 1], "seq", ups)
        ways[1][phase] = lax.ppermute(ways[1][phase - 1], "seq", downs)
        chosen = [orders[i][phase - 1] for i in range(seq)]
        sources = sorted({(way, step) for way, step, origin in chosen})
        index = at_place([jnp.int32(sources.index((way, step))) for way, step, origin in chosen])
        arrival = choose(
            index,
            [ways[way][step] for way, step in sources],
            [last, *before.get(phase + 1, ())],
            WEIGHT if phase == seq - 1 else 0,
        )
        origins.append(at_place([jnp.int32(origin) for way, step, origin in chosen]))

    steps = [place ^ origin for origin in origins]
    by_step = [sum(jnp.where(near == step, i, 0) for i, near in enumerate(steps)) for step in range(seq)]
    order = jnp.concatenate([by_feature, jnp.stack([jnp.int32(i) for i in origins + steps + by_step])])

    far, conv, new_state = finish(order, early, xs, w_keys + w_values, w_queries, decay_rate, residue, carried)
    half = seq // 2
    pieces = {
        step: after(lax.ppermute(far[step - half], "seq", mirror(seq, step)), weight=AHEAD)
        for step in range(half, seq)
    }
    for step, piece in enumerate(gate_near(order, xs, w_queries, conv)):
        pieces[step] = lax.ppermute(piece, "seq", mirror(seq, step)) if step else piece
    pieces = [pieces[step] for step in range(seq)]
    return place_columns(pieces, place), new_state


def solution(mesh):
    in_specs = (
        P(("parts", "seq"), ("chan", "rep")),
        P("seq", ("chan", "rep")),
        P("seq", ("chan", "rep")),
        P("seq", ("chan", "rep")),
        P(("chan", "rep", "seq"), None),
        P(("chan", "rep", "seq"), None),
        P(("parts", "chan", "rep", "seq"), None),
    )
    out_specs = (P(("parts", "seq"), ("chan", "rep")), P(("parts", "chan", "rep", "seq"), None))
    sizes = dict(mesh.shape)

    def program(*arrays):
        tokens = arrays[0]
        part_bytes = tokens.size * tokens.dtype.itemsize * sizes["seq"] * sizes["chan"] * sizes["rep"]
        seq = sizes["seq"]
        fits = part_bytes <= GATHER_BYTES and seq == sizes["chan"] * sizes["rep"]
        fits = fits and seq >= 4 and seq & (seq - 1) == 0
        if fits:
            return by_channels(sizes, *arrays)
        return per_device(*arrays)

    return jax.shard_map(
        program, mesh=mesh, in_specs=in_specs, out_specs=out_specs, check_vma=False
    )
```
